256 devices in a mesh: dp: 32 (over z_hi, x, core), seq: 8 (over y, z_lo).
Axes of the slice: x: 4, y: 4, z: 8 (z_hi: 4, z_lo: 2; z = z_hi * 2 + z_lo), core: 2. Of those that a mesh axis runs over, the one named last changes fastest.
Arguments:
- queries: bfloat16 [32, 1024, 4096], P('dp', 'seq'), may hold values from -6 to 6
- saved_key_state: bfloat16 [32, 1024, 512], P('dp', 'seq'), may hold values from -6 to 6
- saved_value_state: bfloat16 [32, 1024, 512], P('dp', 'seq'), may hold values from -6 to 6
- attn_output: bfloat16 [32, 1024, 4096], P('dp', 'seq'), may hold values from -4 to 4
- grad_output: bfloat16 [32, 1024, 4096], P('dp', 'seq'), may hold values from -6 to 6
- log_denominator: float32 [32, 1024, 32], P('dp', 'seq')
- layer_input: bfloat16 [32, 1024, 5120], P('dp', 'seq'), may hold values from -6 to 6
- doc_lengths: int32 [32, 8], P('dp'), may hold values from 1 to 512, as said below
- image_tiles: int32 [32, 8], P('dp'), may hold values from 0 to 4, as said below
Outputs:
- grad_queries: bfloat16 [32, 1024, 4096], P('dp', 'seq')
- keys_gradient: bfloat16 [32, 1024, 512], P('dp', 'seq')
- values_gradient: bfloat16 [32, 1024, 512], P('dp', 'seq')
- grad_value_weight: float32 [5120, 512], P(('dp', 'seq'))
The draws below stay inside these ranges and needn't reach their ends.
Inputs may be any that keep to these rules, and one draw needn't show every extreme that they name: `doc_lengths`: in every sequence the 8 lengths sum to 1024 and exactly one of them equals 512. `image_tiles`: every sequence has a document with 4 tiles.
All inputs are finite; a program needn't handle non-finite values.
Results may differ from the reference program's by a relative error of at most 0.0059.
Values may be sent and summed in bfloat16 or wider, within the bound.
A program may use at most 128 MiB of HBM per device.

```python
import jax
import jax.numpy as jnp
from jax import lax

D = 5120
HQ = 32
KEY_VALUE_HEADS = 4
HEAD_SIZE = 128
QUERY_PER_KV = 8
NDOC = 8
TILE_TOK = 32
MAX_TILES = 4
SEQUENCE_TOKENS = 1024
SEQUENCE_COUNT = 32
TOKEN_COUNT = 32768


def one_layout(seq_key):
    cut_key, shuffle_key, tile_key, chosen_key = jax.random.split(seq_key, 4)
    longest = SEQUENCE_TOKENS // 2
    remainder = SEQUENCE_TOKENS - longest
    cut_points = jnp.sort(jax.random.permutation(cut_key, remainder - 1)[:NDOC - 2] + 1).astype(jnp.int32)
    boundaries = jnp.concatenate([jnp.zeros((1,), jnp.int32), cut_points, jnp.full((1,), remainder, jnp.int32)])
    others = boundaries[1:] - boundaries[:-1]
    lengths = jnp.concatenate([others, jnp.full((1,), longest, jnp.int32)])
    shuffle = jax.random.permutation(shuffle_key, NDOC)
    lengths = jnp.take(lengths, shuffle).astype(jnp.int32)
    tile_counts = jax.random.randint(tile_key, (NDOC,), 0, MAX_TILES + 1, dtype=jnp.int32)
    chosen = jax.random.randint(chosen_key, (), 0, NDOC, dtype=jnp.int32)
    tile_counts = jnp.where(jnp.arange(NDOC, dtype=jnp.int32) == chosen, MAX_TILES, tile_counts).astype(jnp.int32)
    return (lengths, tile_counts)


def layout(key):
    seq_keys = jax.random.split(key, SEQUENCE_COUNT)
    return jax.vmap(one_layout)(seq_keys)


def count_visible(lengths, tile_counts):
    doc_ends = jnp.cumsum(lengths).astype(jnp.int32)
    doc_starts = doc_ends - lengths
    image_len = jnp.minimum(tile_counts * TILE_TOK, lengths)
    positions = jnp.arange(SEQUENCE_TOKENS, dtype=jnp.int32)
    doc_index = jnp.sum((positions[:, None] >= doc_ends[None, :]).astype(jnp.int32), axis=1)
    picked = doc_index[:, None] == jnp.arange(NDOC, dtype=jnp.int32)[None, :]
    tok_start = jnp.sum(jnp.where(picked, doc_starts[None, :], 0), axis=1)
    tok_image = jnp.sum(jnp.where(picked, image_len[None, :], 0), axis=1)
    return jnp.where(positions < tok_start + tok_image, tok_image, positions - tok_start + 1)


def draw_doc_lengths(key, part):
    lengths, tile_counts = layout(key)
    return lengths


def draw_image_tiles(key, part):
    lengths, tile_counts = layout(key)
    return tile_counts


def draw_log_denominator(key, part):
    lengths, tile_counts = layout(key)
    key = jax.random.fold_in(key, 7)
    visible_count = jax.vmap(count_visible)(lengths, tile_counts)
    baseline = jnp.log(visible_count.astype(jnp.float32)) + 0.5
    jitter = 0.25 * jax.random.truncated_normal(key, -2.0, 2.0, (SEQUENCE_COUNT, SEQUENCE_TOKENS, HQ), jnp.float32)
    return baseline[:, :, None] + jitter


def raised(drawn, rng, source, target, parts, factor):
    def block_of(axis_at):
        return (jnp.arange(drawn.shape[axis_at]) // (drawn.shape[axis_at] // parts)).reshape((-1,) + (1,) * (drawn.ndim - 1 - axis_at))

    first = jax.random.permutation(rng, parts)[block_of(target)]
    second = (block_of(target) + parts // 2) % parts
    return jnp.where((block_of(source) == first) | (block_of(source) == second), factor * drawn, drawn)


def levels(stream_key, dims, pieces, smallest, high):
    def one(position, blocks):
        heights = jax.random.uniform(jax.random.fold_in(jax.random.fold_in(stream_key, 6), position), (blocks,), jnp.float32, smallest / len(pieces), high / len(pieces))
        return jnp.repeat(jnp.exp(heights), dims[position] // blocks).reshape((-1,) + (1,) * (len(dims) - position - 1))

    level = one(*pieces[0])
    for cut in pieces[1:]:
        level = level * one(*cut)
    return level


def gaussian(key, dims, spread, limit, pieces=(), held_as=jnp.bfloat16):
    level = levels(key, dims, pieces, -0.22, 0.18) if pieces else 1.0
    drawn = jax.random.normal(key, dims, jnp.float32) * spread * level
    return jnp.minimum(jnp.maximum(drawn, -limit), limit).astype(held_as)


def bell_draw_with(stream_key, extent, scale, most, shards, heavy, kind=jnp.bfloat16):
    values = scale * jax.random.normal(stream_key, extent, jnp.float32)
    if shards:
        values = values * levels(stream_key, extent, shards, -0.22, 0.18)
    return jnp.clip(raised(values, jax.random.fold_in(stream_key, 3), *heavy), -most, most).astype(kind)


def setup_inputs(seed: int = 0) -> dict:
    keys = jax.random.split(jax.random.key(seed), 10)
    queries = gaussian(keys[0], (SEQUENCE_COUNT, SEQUENCE_TOKENS, HQ * HEAD_SIZE), 1.0, 6.0, ((0, 32), (1, 8)))
    saved_key_state = gaussian(keys[1], (SEQUENCE_COUNT, SEQUENCE_TOKENS, KEY_VALUE_HEADS * HEAD_SIZE), 1.0, 6.0, ((0, 32), (1, 8)))
    saved_value_state = gaussian(keys[2], (SEQUENCE_COUNT, SEQUENCE_TOKENS, KEY_VALUE_HEADS * HEAD_SIZE), 1.0, 6.0, ((0, 32), (1, 8)))
    attn_output = gaussian(keys[3], (SEQUENCE_COUNT, SEQUENCE_TOKENS, HQ * HEAD_SIZE), 0.25, 4.0, ((0, 32), (1, 8)))
    grad_output = gaussian(keys[4], (SEQUENCE_COUNT, SEQUENCE_TOKENS, HQ * HEAD_SIZE), 1.0, 6.0, ((0, 32), (1, 8)))
    log_denominator = draw_log_denominator(jax.random.fold_in(keys[9], 71), 0)
    layer_input = bell_draw_with(keys[6], (SEQUENCE_COUNT, SEQUENCE_TOKENS, D), 1.0, 6.0, ((0, 32), (1, 8)), (1, 2, 8, 2.0))
    doc_lengths = draw_doc_lengths(jax.random.fold_in(keys[9], 71), 0)
    image_tiles = draw_image_tiles(jax.random.fold_in(keys[9], 71), 0)
    return dict(queries=queries, saved_key_state=saved_key_state, saved_value_state=saved_value_state, attn_output=attn_output, grad_output=grad_output, log_denominator=log_denominator, layer_input=layer_input, doc_lengths=doc_lengths, image_tiles=image_tiles)


def token_tables(doc_lengths, image_tiles, seq_length):
    doc_ends = jnp.cumsum(doc_lengths).astype(jnp.int32)
    doc_starts = doc_ends - doc_lengths
    image_ends = doc_starts + jnp.minimum(image_tiles * TILE_TOK, doc_lengths)
    positions = jnp.arange(seq_length, dtype=jnp.int32)
    doc_index = jnp.sum((positions[:, None] >= doc_ends[None, :]).astype(jnp.int32), axis=1)
    picked = doc_index[:, None] == jnp.arange(doc_lengths.shape[0], dtype=jnp.int32)[None, :]
    image_end = jnp.sum(jnp.where(picked, image_ends[None, :], 0), axis=1)
    return doc_index, positions < image_end


def one_sequence(packed):
    queries, saved_key_state, saved_value_state, attn_output, grad_output, log_denominator, doc_lengths, image_tiles = packed
    doc_index, image_flag = token_tables(doc_lengths, image_tiles, SEQUENCE_TOKENS)
    positions = jnp.arange(SEQUENCE_TOKENS, dtype=jnp.int32)
    visible = (doc_index[:, None] == doc_index[None, :]) & ((positions[None, :] <= positions[:, None]) | (image_flag[:, None] & image_flag[None, :]))
    score_scale = HEAD_SIZE ** -0.5
    query_heads = queries.reshape(SEQUENCE_TOKENS, HQ, HEAD_SIZE).transpose(1, 0, 2)
    grad_heads = grad_output.reshape(SEQUENCE_TOKENS, HQ, HEAD_SIZE).transpose(1, 0, 2)
    output_heads = attn_output.reshape(SEQUENCE_TOKENS, HQ, HEAD_SIZE).transpose(1, 0, 2)
    stat_heads = log_denominator.T
    heads_of_key = saved_key_state.reshape(SEQUENCE_TOKENS, KEY_VALUE_HEADS, HEAD_SIZE).transpose(1, 0, 2)
    heads_of_value = saved_value_state.reshape(SEQUENCE_TOKENS, KEY_VALUE_HEADS, HEAD_SIZE).transpose(1, 0, 2)
    kv_index = jnp.arange(HQ, dtype=jnp.int32) // QUERY_PER_KV

    def one_head(packed_head):
        query_one, grad_one, output_one, stat_one, kv_one = packed_head
        key_one = heads_of_key[kv_one]
        value_one = heads_of_value[kv_one]
        scores = jnp.dot(query_one, key_one.T, preferred_element_type=jnp.float32) * score_scale
        attn_probs = jnp.where(visible, jnp.exp(scores - stat_one[:, None]), 0.0)
        grad_probs = jnp.dot(grad_one, value_one.T, preferred_element_type=jnp.float32)
        row_delta = jnp.sum(grad_one.astype(jnp.float32) * output_one.astype(jnp.float32), axis=1)
        grad_scores = attn_probs * (grad_probs - row_delta[:, None])
        probs_bf = attn_probs.astype(jnp.bfloat16)
        scores_bf = grad_scores.astype(jnp.bfloat16)
        grad_query = (jnp.dot(scores_bf, key_one, preferred_element_type=jnp.float32) * score_scale).astype(jnp.bfloat16)
        key_gradient = jnp.dot(scores_bf.T, query_one, preferred_element_type=jnp.float32) * score_scale
        value_gradient = jnp.dot(probs_bf.T, grad_one, preferred_element_type=jnp.float32)
        return grad_query, key_gradient, value_gradient

    grad_query, key_gradient, value_gradient = lax.map(one_head, (query_heads, grad_heads, output_heads, stat_heads, kv_index))
    grad_queries = grad_query.transpose(1, 0, 2).reshape(SEQUENCE_TOKENS, HQ * HEAD_SIZE)
    keys_gradient = jnp.sum(key_gradient.reshape(KEY_VALUE_HEADS, QUERY_PER_KV, SEQUENCE_TOKENS, HEAD_SIZE), axis=1).astype(jnp.bfloat16)
    values_gradient = jnp.sum(value_gradient.reshape(KEY_VALUE_HEADS, QUERY_PER_KV, SEQUENCE_TOKENS, HEAD_SIZE), axis=1).astype(jnp.bfloat16)
    keys_gradient = keys_gradient.transpose(1, 0, 2).reshape(SEQUENCE_TOKENS, KEY_VALUE_HEADS * HEAD_SIZE)
    values_gradient = values_gradient.transpose(1, 0, 2).reshape(SEQUENCE_TOKENS, KEY_VALUE_HEADS * HEAD_SIZE)
    return grad_queries, keys_gradient, values_gradient


def reference(queries, saved_key_state, saved_value_state, attn_output, grad_output, log_denominator, layer_input, doc_lengths, image_tiles):
    grad_queries, keys_gradient, values_gradient = lax.map(one_sequence, (queries, saved_key_state, saved_value_state, attn_output, grad_output, log_denominator, doc_lengths, image_tiles))
    flat_input = layer_input.reshape(TOKEN_COUNT, D)
    values_flattened = values_gradient.reshape(TOKEN_COUNT, KEY_VALUE_HEADS * HEAD_SIZE)
    grad_value_weight = jnp.dot(flat_input.T, values_flattened, preferred_element_type=jnp.float32) * (TOKEN_COUNT ** -0.5)
    return grad_queries, keys_gradient, values_gradient, grad_value_weight
```

```python
import functools
import math

import jax
import jax.numpy as jnp
from jax import lax
from jax.experimental import pallas as pl
from jax.experimental.pallas import tpu as pltpu
from jax.sharding import PartitionSpec as P

HQ = 32
KV = 4
HEAD = 128
GROUP = HQ // KV
TILE_TOK = 32
TOK = 128
CORES = 2
SCALE = HEAD ** -0.5
LOG2E = math.log2(math.e)
HIDDEN = -1e30
REL = (0, 1, -1, -2, -3, -4)
NT = (((1,), (1,)), ((), ()))


def kernel(
    nx, nz, ns, doc_ref, tiles_ref, q_hbm, k_hbm, v_hbm, o_hbm, do_hbm, lse_hbm, x_hbm,
    dq_hbm, dk_hbm, dv_hbm, dw_hbm,
    q_s, o_s, do_s, lse_s, x_s, kvb, bias, lse_t, dq_s, own, sb, rb, dkv,
    x_t, xg, xp, dvall, wf, st1, r1, acc, st2, r2, out_s,
    ld_kv, ld, out_sem, kv_ss, kv_rs, pg_ss, pg_rs, x_ss, x_rs, ag_ss, ag_rs, rs_ss, rs_rs, z_ss, z_rs,
):
    nxc = nx * CORES
    d = lax.axis_index("dp")
    s = lax.axis_index("seq")
    zh = d // nxc
    i = lax.rem(d, nxc)
    xc = i // CORES
    core = lax.rem(i, CORES)
    rows = wf.shape[1]
    part = rows // ns
    own_rows = part // nz

    def remote(src, dst, ss, rs, **where):
        return pltpu.make_async_remote_copy(
            src_ref=src, dst_ref=dst, send_sem=ss, recv_sem=rs, device_id=where,
            device_id_type=pl.DeviceIdType.MESH,
        )

    def inside(t):
        return (t >= 0) & (t < ns)

    def wrap(t):
        return lax.rem(t + ns, ns)

    for g in range(KV):
        pltpu.make_async_copy(k_hbm.at[:, pl.ds(g * HEAD, HEAD)], kvb.at[0, g, 0], ld_kv.at[g, 0]).start()
        pltpu.make_async_copy(v_hbm.at[:, pl.ds(g * HEAD, HEAD)], kvb.at[0, g, 1], ld_kv.at[g, 1]).start()
    loads = [
        pltpu.make_async_copy(src, dst, ld.at[n])
        for n, (src, dst) in enumerate(
            ((x_hbm, x_s), (do_hbm, do_s), (o_hbm, o_s), (q_hbm, q_s), (lse_hbm, lse_s))
        )
    ]
    for copy in loads:
        copy.start()
    for c in range(1, len(REL)):
        @pl.when(jnp.logical_not(inside(s + REL[c])))
        def _():
            kvb[c] = jnp.zeros(kvb.shape[1:], kvb.dtype)

    barrier = pltpu.get_barrier_semaphore()
    peers = [dict(seq=wrap(s + m)) for m in range(1, ns)]
    peers += [dict(dp=zh * nxc + lax.rem(i + m, nxc)) for m in range(1, nxc)]
    peers += [dict(dp=lax.rem(zh + m, nz) * nxc + i) for m in range(1, nz)]
    for peer in peers:
        pl.semaphore_signal(barrier, inc=1, device_id=peer, device_id_type=pl.DeviceIdType.MESH)
    pl.semaphore_wait(barrier, len(peers))

    def kv_copy(g, c):
        return remote(
            kvb.at[0, g], kvb.at[c, g], kv_ss.at[c - 1, g], kv_rs.at[c - 1, g], seq=wrap(s - REL[c])
        )

    def pg_copy(g, c):
        return remote(
            sb.at[c - 1, g], rb.at[c - 1, g], pg_ss.at[c - 1, g], pg_rs.at[c - 1, g], seq=wrap(s + REL[c])
        )

    for g in range(KV):
        for half in range(2):
            src = (k_hbm, v_hbm)[half]
            pltpu.make_async_copy(src.at[:, pl.ds(g * HEAD, HEAD)], kvb.at[0, g, half], ld_kv.at[g, half]).wait()
        for c in range(1, len(REL)):
            @pl.when(inside(s - REL[c]))
            def _():
                kv_copy(g, c).start()

    loads[0].wait()
    slab = rows // nz
    for tile in range(x_s.shape[1] // TOK):
        turned = x_s[:, tile * TOK:(tile + 1) * TOK].T
        at = tile * TOK
        while at < (tile + 1) * TOK:
            block, offset = divmod(at, slab)
            length = min((tile + 1) * TOK - at, slab - offset)
            lead = at - tile * TOK
            x_t[block // nxc, block % nxc, offset:offset + length, :] = turned[lead:lead + length, :]
            at += length

    def x_copy(m):
        j = lax.rem(i + m, nxc)
        return remote(x_t.at[:, j], xg.at[i], x_ss.at[m - 1], x_rs.at[m - 1], dp=zh * nxc + j)

    for m in range(1, nxc):
        x_copy(m).start()
    xg[i] = x_t[:, i]

    row = s * TOK + lax.broadcasted_iota(jnp.int32, (1, TOK), 1)
    low = jnp.zeros((1, TOK), jnp.int32)
    high = jnp.zeros((1, TOK), jnp.int32)
    start = jnp.int32(0)
    for n in range(doc_ref.shape[1]):
        length = doc_ref[0, n]
        image_end = start + jnp.minimum(tiles_ref[0, n] * TILE_TOK, length)
        here = row >= start
        low = jnp.where(here, start, low)
        high = jnp.where(here, image_end, high)
        start = start + length
    high = jnp.maximum(row + 1, high)
    for c in range(len(REL)):
        key = (s + REL[c]) * TOK + lax.broadcasted_iota(jnp.int32, (TOK, TOK), 0)
        tile = jnp.where((key >= low) & (key < high), 0.0, HIDDEN).astype(jnp.float32)
        p, half = divmod(c, 2)
        bias[p, half * TOK:(half + 1) * TOK, :TOK] = tile
        bias[p, half * TOK:(half + 1) * TOK, TOK:] = tile
    loads[4].wait()
    lse_t[...] = lse_s[...].T * LOG2E
    for copy in loads[1:4]:
        copy.wait()

    head_lane = lax.broadcasted_iota(jnp.int32, (GROUP, GROUP * HEAD), 1)
    head_row = lax.broadcasted_iota(jnp.int32, (GROUP, GROUP * HEAD), 0)
    picks = ((head_lane >= head_row * HEAD) & (head_lane < (head_row + 1) * HEAD)).astype(jnp.bfloat16)

    def dq_copy(g):
        cols = pl.ds(g * GROUP * HEAD, GROUP * HEAD)
        return pltpu.make_async_copy(dq_s.at[:, cols], dq_hbm.at[:, cols], out_sem.at[g])

    def attend(g, carry):
        base = g * GROUP * HEAD

        def heads(ref):
            return jnp.concatenate([ref[:, pl.ds(base + h * HEAD, HEAD)] for h in range(GROUP)], axis=0)

        wide = pl.ds(base, GROUP * HEAD)
        product = do_s[:, wide].astype(jnp.float32) * o_s[:, wide].astype(jnp.float32)
        coarse = product.astype(jnp.bfloat16)
        fine = (product - coarse.astype(jnp.float32)).astype(jnp.bfloat16)
        delta = lax.dot_general(picks, coarse, NT, preferred_element_type=jnp.float32)
        delta += lax.dot_general(picks, fine, NT, preferred_element_type=jnp.float32)
        stat = lse_t[pl.ds(pl.multiple_of(g * GROUP, GROUP), GROUP), :]
        q8, do8 = heads(q_s), heads(do_s)
        total = None
        for p in range(len(REL) // 2):
            for c in (2 * p, 2 * p + 1):
                if c:
                    @pl.when(inside(s + REL[c]))
                    def _():
                        kv_copy(g, c).wait_recv()
            keys = jnp.concatenate([kvb[2 * p, g, 0], kvb[2 * p + 1, g, 0]], axis=0)
            values = jnp.concatenate([kvb[2 * p, g, 1], kvb[2 * p + 1, g, 1]], axis=0)
            probs, steps = [], []
            for pair in range(GROUP // 2):
                cut = slice(pair * 2 * TOK, (pair + 1) * 2 * TOK)
                two = [pair * 2, pair * 2 + 1]
                stat_row = jnp.concatenate([stat[h:h + 1] for h in two], axis=1)
                delta_row = jnp.concatenate([delta[h:h + 1] for h in two], axis=1)
                scores = lax.dot_general(keys, q8[cut], NT, preferred_element_type=jnp.float32)
                prob = jnp.exp2(scores * (SCALE * LOG2E) - stat_row + bias[p])
                grad = lax.dot_general(values, do8[cut], NT, preferred_element_type=jnp.float32)
                probs.append(prob.astype(jnp.bfloat16))
                steps.append((prob * (grad - delta_row)).astype(jnp.bfloat16))
            probs = jnp.concatenate(probs, axis=1)
            steps = jnp.concatenate(steps, axis=1)
            dv = jnp.dot(probs, do8, preferred_element_type=jnp.float32)
            dk = jnp.dot(steps, q8, preferred_element_type=jnp.float32) * SCALE
            dq = jnp.dot(keys.T, steps, preferred_element_type=jnp.float32)
            total = dq if total is None else total + dq
            for c in (2 * p, 2 * p + 1):
                half = slice((c - 2 * p) * TOK, (c - 2 * p + 1) * TOK)
                if c == 0:
                    own[g, 0] = dk[half]
                    own[g, 1] = dv[half]
                else:
                    sb[c - 1, g, 0] = dk[half].astype(jnp.bfloat16)
                    sb[c - 1, g, 1] = dv[half].astype(jnp.bfloat16)

                    @pl.when(inside(s + REL[c]))
                    def _():
                        pg_copy(g, c).start()
        for h in range(GROUP):
            dq_s[:, pl.ds(base + h * HEAD, HEAD)] = (
                total[:, h * TOK:(h + 1) * TOK].T * SCALE
            ).astype(jnp.bfloat16)
        dq_copy(g).start()
        return carry

    lax.fori_loop(0, KV, attend, 0)

    old = lax.broadcasted_iota(jnp.int32, (1, rows), 1)
    new = old
    before = 0
    for n in range(1, nz * ns):
        shift = (n % ns * nz + n // ns - n) * own_rows
        new = new + jnp.where(old >= n * own_rows, shift - before, 0)
        before = shift
    order = (lax.broadcasted_iota(jnp.int32, (rows, rows), 0) == new).astype(jnp.bfloat16)
    for m in range(1, nxc):
        x_copy(m).wait_recv()

    def reorder(jj, carry):
        two = jnp.concatenate([xg[2 * jj].reshape(rows, TOK), xg[2 * jj + 1].reshape(rows, TOK)], axis=1)
        xp[:, pl.ds(pl.multiple_of(jj * 2 * TOK, 2 * TOK), 2 * TOK)] = jnp.dot(
            order, two, preferred_element_type=jnp.float32
        ).astype(jnp.bfloat16)
        return carry

    lax.fori_loop(0, nxc // 2, reorder, 0)

    def ag_copy(g, j, n, **where):
        return remote(dvall.at[g, j], dvall.at[g, j], ag_ss.at[g, n], ag_rs.at[g, j], **where)

    sibling = (zh * nx + xc) * CORES + 1 - core

    def along_x(m):
        return lax.rem(xc + m, nx)

    def settle(g, carry):
        for c in range(1, len(REL)):
            @pl.when(inside(s - REL[c]))
            def _():
                pg_copy(g, c).wait_recv()
                own[g] += rb[c - 1, g].astype(jnp.float32)
        done = own[g].astype(jnp.bfloat16)
        cols = pl.ds(pl.multiple_of(g * HEAD, HEAD), HEAD)
        dkv[0, :, cols] = done[0]
        dkv[1, :, cols] = done[1]
        dvall[g, i] = done[1]
        for m in range(1, nx):
            ag_copy(g, i, m - 1, dp=(zh * nx + along_x(m)) * CORES + core).start()
        ag_copy(g, i, nx - 1, dp=sibling).start()
        return carry

    lax.fori_loop(0, KV, settle, 0)
    out_k = pltpu.make_async_copy(dkv.at[0], dk_hbm, out_sem.at[KV])
    out_v = pltpu.make_async_copy(dkv.at[1], dv_hbm, out_sem.at[KV + 1])
    out_k.start()
    out_v.start()

    def relay(g, carry):
        for m in range(1, nx):
            j = along_x(m) * CORES + core
            ag_copy(g, j, nx - 1 + m, dp=sibling).wait_recv()
            ag_copy(g, j, nx - 1 + m, dp=sibling).start()
        return carry

    lax.fori_loop(0, KV, relay, 0)

    def rs_copy(g, m):
        to = wrap(s + m)
        return remote(st1.at[g, to], r1.at[g, m - 1], rs_ss.at[g, m - 1], rs_rs.at[g, m - 1], seq=to)

    def weight(g, carry):
        for m in range(nx):
            j = along_x(m) * CORES + 1 - core
            ag_copy(g, j, 0, dp=sibling).wait_recv()
        values = dvall[g].reshape(nxc * TOK, HEAD)
        product = jnp.dot(xp[...], values, preferred_element_type=jnp.float32)
        wf[g] = product
        st1[g] = product.astype(jnp.bfloat16).reshape(ns, part, HEAD)
        for m in range(1, ns):
            rs_copy(g, m).start()
        return carry

    lax.fori_loop(0, KV, weight, 0)

    st2[...] = jnp.zeros(st2.shape, st2.dtype)

    def gather_rows(g, carry):
        mine = wf[g, pl.ds(pl.multiple_of(s * part, part), part), :]
        for m in range(1, ns):
            rs_copy(g, m).wait_recv()
            mine = mine + r1[g, m - 1].astype(jnp.float32)
        acc[:, pl.ds(pl.multiple_of(g * HEAD, HEAD), HEAD)] = mine
        return carry

    lax.fori_loop(0, KV, gather_rows, 0)
    for n in range(nz):
        st2[n, :own_rows, :] = acc[n * own_rows:(n + 1) * own_rows, :]

    def z_copy(m):
        to = lax.rem(zh + m, nz)
        return remote(st2.at[to], r2.at[m - 1], z_ss.at[m - 1], z_rs.at[m - 1], dp=to * nxc + i)

    for m in range(1, nz):
        z_copy(m).start()
    result = st2[zh, :own_rows, :]
    for m in range(1, nz):
        z_copy(m).wait_recv()
        result = result + r2[m - 1, :own_rows, :]
    out_s[...] = result * ((ns * nz * nxc * TOK) ** -0.5)
    out_w = pltpu.make_async_copy(out_s, dw_hbm, out_sem.at[KV + 2])
    out_w.start()

    def drain(g, carry):
        for c in range(1, len(REL)):
            @pl.when(inside(s - REL[c]))
            def _():
                kv_copy(g, c).wait_send()

            @pl.when(inside(s + REL[c]))
            def _():
                pg_copy(g, c).wait_send()
        for m in range(1, nx):
            ag_copy(g, i, m - 1, dp=sibling).wait_send()
            ag_copy(g, i, nx - 1 + m, dp=sibling).wait_send()
        ag_copy(g, i, nx - 1, dp=sibling).wait_send()
        for m in range(1, ns):
            rs_copy(g, m).wait_send()
        dq_copy(g).wait()
        return carry

    lax.fori_loop(0, KV, drain, 0)
    for m in range(1, nxc):
        x_copy(m).wait_send()
    for m in range(1, nz):
        z_copy(m).wait_send()
    out_k.wait()
    out_v.wait()
    out_w.wait()


def solution(mesh, nx=4):
    ns = mesh.shape["seq"]
    nxc = nx * CORES
    nz = mesh.shape["dp"] // nxc

    def on_device(q, k, v, o, do, lse, x, docs, tiles):
        width = x.shape[2]
        own_rows = width // (ns * nz * nxc)
        part = own_rows * nz
        rows = part * ns
        padded = -(-own_rows // 8) * 8
        slots = len(REL)
        bf, f32 = jnp.bfloat16, jnp.float32
        hbm = pl.BlockSpec(memory_space=pl.ANY)
        smem = pl.BlockSpec(memory_space=pltpu.SMEM)
        dma = pltpu.SemaphoreType.DMA
        scratch = [
            pltpu.VMEM((TOK, HQ * HEAD), bf),
            pltpu.VMEM((TOK, HQ * HEAD), bf),
            pltpu.VMEM((TOK, HQ * HEAD), bf),
            pltpu.VMEM((TOK, HQ), f32),
            pltpu.VMEM((TOK, width), bf),
            pltpu.VMEM((slots, KV, 2, TOK, HEAD), bf),
            pltpu.VMEM((slots // 2, 2 * TOK, 2 * TOK), f32),
            pltpu.VMEM((HQ, TOK), f32),
            pltpu.VMEM((TOK, HQ * HEAD), bf),
            pltpu.VMEM((KV, 2, TOK, HEAD), f32),
            pltpu.VMEM((slots - 1, KV, 2, TOK, HEAD), bf),
            pltpu.VMEM((slots - 1, KV, 2, TOK, HEAD), bf),
            pltpu.VMEM((2, TOK, KV * HEAD), bf),
            pltpu.VMEM((nz, nxc, rows // nz, TOK), bf),
            pltpu.VMEM((nxc, nz, rows // nz, TOK), bf),
            pltpu.VMEM((rows, nxc * TOK), bf),
            pltpu.VMEM((KV, nxc, TOK, HEAD), bf),
            pltpu.VMEM((KV, rows, HEAD), f32),
            pltpu.VMEM((KV, ns, part, HEAD), bf),
            pltpu.VMEM((KV, ns - 1, part, HEAD), bf),
            pltpu.VMEM((part, KV * HEAD), f32),
            pltpu.VMEM((nz, padded, KV * HEAD), f32),
            pltpu.VMEM((max(nz - 1, 1), padded, KV * HEAD), f32),
            pltpu.VMEM((own_rows, KV * HEAD), f32),
            dma((KV, 2)),
            dma((5,)),
            dma((KV + 3,)),
            dma((slots - 1, KV)),
            dma((slots - 1, KV)),
            dma((slots - 1, KV)),
            dma((slots - 1, KV)),
            dma((nxc - 1,)),
            dma((nxc - 1,)),
            dma((KV, 2 * nx - 1)),
            dma((KV, nxc)),
            dma((KV, ns - 1)),
            dma((KV, ns - 1)),
            dma((max(nz - 1, 1),)),
            dma((max(nz - 1, 1),)),
        ]
        dq, dk, dv, dw = pl.pallas_call(
            functools.partial(kernel, nx, nz, ns),
            out_shape=(
                jax.ShapeDtypeStruct((TOK, HQ * HEAD), bf),
                jax.ShapeDtypeStruct((TOK, KV * HEAD), bf),
                jax.ShapeDtypeStruct((TOK, KV * HEAD), bf),
                jax.ShapeDtypeStruct((own_rows, KV * HEAD), f32),
            ),
            in_specs=[smem, smem] + [hbm] * 7,
            out_specs=(hbm,) * 4,
            scratch_shapes=scratch,
            compiler_params=pltpu.CompilerParams(
                collective_id=0, has_side_effects=True, vmem_limit_bytes=48 * 2**20
            ),
        )(docs, tiles, q[0], k[0], v[0], o[0], do[0], lse[0], x[0])
        return dq[None], dk[None], dv[None], dw

    split = P("dp", "seq", None)
    return jax.shard_map(
        on_device,
        mesh=mesh,
        in_specs=(split,) * 7 + (P("dp", None),) * 2,
        out_specs=(split,) * 3 + (P(("dp", "seq"), None),),
        check_vma=False,
    )
```

```python
import functools
import math

import jax
import jax.numpy as jnp
from jax import lax
from jax.experimental import pallas as pl
from jax.experimental.pallas import tpu as pltpu
from jax.sharding import PartitionSpec as P

HQ = 32
KV = 4
HEAD = 128
GROUP = HQ // KV
TILE_TOK = 32
TOK = 128
CORES = 2
SCALE = HEAD ** -0.5
LOG2E = math.log2(math.e)
HIDDEN = -1e30
REL = (0, 1, -1, -2, -3, -4)
NT = (((1,), (1,)), ((), ()))


def kernel(
    nx, nz, ns, doc_ref, tiles_ref, q_hbm, k_hbm, v_hbm, o_hbm, do_hbm, lse_hbm, x_hbm,
    dq_hbm, dk_hbm, dv_hbm, dw_hbm,
    q_s, o_s, do_s, x_s, kvb, bias, lse_t, delta_s, prob_s, dq_s, own, mid, sb, rb, dkv,
    x_t, xg, xp, dvall, wf, st1, r1, acc, st2, r2, out_s,
    ld_kv, ld, out_sem, kv_ss, kv_rs, pg_ss, pg_rs, x_ss, x_rs, ag_ss, ag_rs, rs_ss, rs_rs, z_ss, z_rs,
):
    nxc = nx * CORES
    d = lax.axis_index("dp")
    s = lax.axis_index("seq")
    zh = d // nxc
    i = lax.rem(d, nxc)
    xc = i // CORES
    core = lax.rem(i, CORES)
    rows = wf.shape[1]
    part = rows // ns
    own_rows = part // nz

    def remote(src, dst, ss, rs, **where):
        return pltpu.make_async_remote_copy(
            src_ref=src, dst_ref=dst, send_sem=ss, recv_sem=rs, device_id=where,
            device_id_type=pl.DeviceIdType.MESH,
        )

    def inside(t):
        return (t >= 0) & (t < ns)

    def wrap(t):
        return lax.rem(t + ns, ns)

    barrier = pltpu.get_barrier_semaphore()
    peers = [dict(seq=wrap(s + m)) for m in range(1, ns)]
    peers += [dict(dp=zh * nxc + lax.rem(i + m, nxc)) for m in range(1, nxc)]
    peers += [dict(dp=lax.rem(zh + m, nz) * nxc + i) for m in range(1, nz)]
    for peer in peers:
        pl.semaphore_signal(barrier, inc=1, device_id=peer, device_id_type=pl.DeviceIdType.MESH)

    def kv_load(g, half):
        src = (k_hbm, v_hbm)[half]
        return pltpu.make_async_copy(src.at[:, pl.ds(g * HEAD, HEAD)], kvb.at[0, g, half], ld_kv.at[g, half])

    for g in range(KV):
        kv_load(g, 0).start()
        kv_load(g, 1).start()
    loads = [
        pltpu.make_async_copy(src, dst, ld.at[n])
        for n, (src, dst) in enumerate(
            ((x_hbm, x_s), (do_hbm, do_s), (o_hbm, o_s), (q_hbm, q_s), (lse_hbm, lse_t))
        )
    ]
    for copy in loads:
        copy.start()
    for c in range(1, len(REL)):
        @pl.when(jnp.logical_not(inside(s + REL[c])))
        def _():
            kvb[c] = jnp.zeros(kvb.shape[1:], kvb.dtype)
    st2[...] = jnp.zeros(st2.shape, st2.dtype)

    z = lax.rem(s, 2)

    def kv_copy(g, n, half):
        held, slot, to, wanted = (
            (0, 2 - z, s + 1 - 2 * z, True),
            (0, 3, s + 2, True),
            (3, 5, s + 2, inside(s - 2)),
            (1 + z, 2 + 2 * z, s + 2, True),
            (2, 1, s - 2, z == 1),
            (5, 4, s - 1, (z == 1) & inside(s - 4)),
        )[n]
        copy = remote(
            kvb.at[held, g, half], kvb.at[slot, g, half], kv_ss.at[n, g, half], kv_rs.at[slot - 1, g, half],
            seq=wrap(to),
        )
        return copy, inside(to) & wanted

    def kv_send(g, n, half):
        copy, wanted = kv_copy(g, n, half)

        @pl.when(wanted)
        def _():
            copy.start()

    def kv_arrived(g, c, half):
        remote(
            kvb.at[0, g, half], kvb.at[c, g, half], kv_ss.at[0, g, half], kv_rs.at[c - 1, g, half],
            seq=wrap(s + 1),
        ).wait_recv()

    def pg_copy(g, c, half):
        to = s - 2 if c >= 4 else s + REL[c]
        copy = remote(
            sb.at[c - 1, g, half], rb.at[c - 1, g, half], pg_ss.at[c - 1, g, half], pg_rs.at[c - 1, g, half],
            seq=wrap(to),
        )
        return copy, inside(s + REL[c])

    def pg_send(g, c, half):
        copy, wanted = pg_copy(g, c, half)

        @pl.when(wanted)
        def _():
            copy.start()

    def pg_from(c):
        return inside(s + 2) & inside(s + 2 + REL[c]) if c >= 4 else inside(s - REL[c])

    loads[0].wait()
    slab = rows // nz
    for tile in range(x_s.shape[1] // TOK):
        turned = x_s[:, tile * TOK:(tile + 1) * TOK].T
        at = tile * TOK
        while at < (tile + 1) * TOK:
            block, offset = divmod(at, slab)
            length = min((tile + 1) * TOK - at, slab - offset)
            lead = at - tile * TOK
            x_t[block // nxc, block % nxc, offset:offset + length, :] = turned[lead:lead + length, :]
            at += length

    def x_copy(m):
        j = lax.rem(i + m, nxc)
        return remote(x_t.at[:, j], xg.at[i], x_ss.at[m - 1], x_rs.at[m - 1], dp=zh * nxc + j)

    xg[i] = x_t[:, i]

    row = s * TOK + lax.broadcasted_iota(jnp.int32, (1, TOK), 1)
    low = jnp.zeros((1, TOK), jnp.int32)
    high = jnp.zeros((1, TOK), jnp.int32)
    start = jnp.int32(0)
    for n in range(doc_ref.shape[1]):
        length = doc_ref[0, n]
        image_end = start + jnp.minimum(tiles_ref[0, n] * TILE_TOK, length)
        here = row >= start
        low = jnp.where(here, start, low)
        high = jnp.where(here, image_end, high)
        start = start + length
    high = jnp.maximum(row + 1, high)
    for c in range(len(REL)):
        key = (s + REL[c]) * TOK + lax.broadcasted_iota(jnp.int32, (TOK, TOK), 0)
        tile = jnp.where((key >= low) & (key < high), 0.0, HIDDEN).astype(jnp.float32)
        p, half = divmod(c, 2)
        bias[p, half * TOK:(half + 1) * TOK, :TOK] = tile
        bias[p, half * TOK:(half + 1) * TOK, TOK:] = tile
    for g in range(KV):
        kv_load(g, 0).wait()
        kv_load(g, 1).wait()
    pl.semaphore_wait(barrier, len(peers))
    def send_own(half):
        for g in range(KV):
            kv_send(g, 0, half)
            kv_send(g, 1, half)

    send_own(0)
    for m in range(1, nxc):
        x_copy(m).start()
    for copy in loads[1:]:
        copy.wait()

    head_lane = lax.broadcasted_iota(jnp.int32, (GROUP, GROUP * HEAD), 1)
    head_row = lax.broadcasted_iota(jnp.int32, (GROUP, GROUP * HEAD), 0)
    picks = ((head_lane >= head_row * HEAD) & (head_lane < (head_row + 1) * HEAD)).astype(jnp.bfloat16)

    def dq_copy(g):
        cols = pl.ds(g * GROUP * HEAD, GROUP * HEAD)
        return pltpu.make_async_copy(dq_s.at[:, cols], dq_hbm.at[:, cols], out_sem.at[g])

    def group_rows(g):
        return pl.ds(pl.multiple_of(g * GROUP, GROUP), GROUP)

    def row_delta(g, carry):
        wide = pl.ds(pl.multiple_of(g * GROUP * HEAD, GROUP * HEAD), GROUP * HEAD)
        product = do_s[:, wide].astype(jnp.float32) * o_s[:, wide].astype(jnp.float32)
        coarse = product.astype(jnp.bfloat16)
        fine = (product - coarse.astype(jnp.float32)).astype(jnp.bfloat16)
        delta = lax.dot_general(picks, coarse, NT, preferred_element_type=jnp.float32)
        delta += lax.dot_general(picks, fine, NT, preferred_element_type=jnp.float32)
        delta_s[group_rows(g), :] = delta
        return carry

    lax.fori_loop(0, KV, row_delta, 0)

    def forward(half, g):
        @pl.when(z == 0)
        def _():
            kv_arrived(g, 1, half)

        @pl.when(z == 1)
        def _():
            kv_arrived(g, 2, half)

        kv_send(g, 3, half)
        kv_send(g, 4, half)

        @pl.when(inside(s - 2))
        def _():
            kv_arrived(g, 3, half)

        kv_send(g, 2, half)

    def forward_keys(g, carry):
        forward(0, g)
        return carry

    lax.fori_loop(0, KV, forward_keys, 0)
    send_own(1)

    def heads(ref, g):
        return jnp.concatenate([ref[:, pl.ds((g * GROUP + h) * HEAD, HEAD)] for h in range(GROUP)], axis=0)

    def await_blocks(g, p, half):
        awaited = (
            ((1, z == 1),),
            ((5, z == 1), (2, z == 0)),
            ((4, z >= 0), (5, z == 0)),
        )[p]
        for c, here in awaited:
            @pl.when(inside(s + REL[c]) & here)
            def _():
                kv_arrived(g, c, half)

            if p == 1 and c == 5:
                kv_send(g, 5, half)
        return jnp.concatenate([kvb[2 * p, g, half], kvb[2 * p + 1, g, half]], axis=0)

    def keep(g, p, half, partial):
        for c in (2 * p, 2 * p + 1):
            block = partial[(c - 2 * p) * TOK:(c - 2 * p + 1) * TOK]
            if c == 0:
                own[g, half] = block
            elif c in (2, 3):
                mid[c - 2, g, half] = block
            else:
                sb[c - 1, g, half] = block.astype(jnp.bfloat16)
                pg_send(g, c, half)

    pairs = [(n, slice(n * 2 * TOK, (n + 1) * 2 * TOK)) for n in range(GROUP // 2)]

    def two_rows(stat, n):
        return jnp.concatenate([stat[2 * n:2 * n + 1], stat[2 * n + 1:2 * n + 2]], axis=1)

    def attend_values(g):
        stat = lse_t[group_rows(g), :] * LOG2E
        q8, do8 = heads(q_s, g), heads(do_s, g)
        for p in range(len(REL) // 2):
            keys = await_blocks(g, p, 0)
            probs = []
            for n, cut in pairs:
                scores = lax.dot_general(keys, q8[cut], NT, preferred_element_type=jnp.float32)
                prob = jnp.exp2(scores * (SCALE * LOG2E) - two_rows(stat, n) + bias[p])
                prob_s[g, p, :, cut] = prob
                probs.append(prob.astype(jnp.bfloat16))
            probs = jnp.concatenate(probs, axis=1)
            keep(g, p, 1, jnp.dot(probs, do8, preferred_element_type=jnp.float32))

    def attend_keys(g):
        delta = delta_s[group_rows(g), :]
        q8, do8 = heads(q_s, g), heads(do_s, g)
        total = None
        for p in range(len(REL) // 2):
            values = await_blocks(g, p, 1)
            keys = jnp.concatenate([kvb[2 * p, g, 0], kvb[2 * p + 1, g, 0]], axis=0)
            steps = []
            for n, cut in pairs:
                grad = lax.dot_general(values, do8[cut], NT, preferred_element_type=jnp.float32)
                steps.append((prob_s[g, p, :, cut] * (grad - two_rows(delta, n))).astype(jnp.bfloat16))
            steps = jnp.concatenate(steps, axis=1)
            keep(g, p, 0, jnp.dot(steps, q8, preferred_element_type=jnp.float32) * SCALE)
            dq = jnp.dot(keys.T, steps, preferred_element_type=jnp.float32)
            total = dq if total is None else total + dq
        for h in range(GROUP):
            dq_s[:, pl.ds((g * GROUP + h) * HEAD, HEAD)] = (
                total[:, h * TOK:(h + 1) * TOK].T * SCALE
            ).astype(jnp.bfloat16)
        dq_copy(g).start()

    def reorder_columns():
        old = lax.broadcasted_iota(jnp.int32, (1, rows), 1)
        new = old
        before = 0
        for n in range(1, nz * ns):
            shift = (n % ns * nz + n // ns - n) * own_rows
            new = new + jnp.where(old >= n * own_rows, shift - before, 0)
            before = shift
        order = (lax.broadcasted_iota(jnp.int32, (rows, rows), 0) == new).astype(jnp.bfloat16)
        for m in range(1, nxc):
            x_copy(m).wait_recv()

        def reorder(jj, carry):
            two = jnp.concatenate([xg[2 * jj].reshape(rows, TOK), xg[2 * jj + 1].reshape(rows, TOK)], axis=1)
            xp[:, pl.ds(pl.multiple_of(jj * 2 * TOK, 2 * TOK), 2 * TOK)] = jnp.dot(
                order, two, preferred_element_type=jnp.float32
            ).astype(jnp.bfloat16)
            return carry

        lax.fori_loop(0, nxc // 2, reorder, 0)

    def ag_copy(g, m):
        to = lax.rem(i + m, nxc)
        return remote(
            dvall.at[g, i], dvall.at[g, i], ag_ss.at[g, m - 1], ag_rs.at[g, m - 1], dp=zh * nxc + to
        )

    def group_cols(g):
        return pl.ds(pl.multiple_of(g * HEAD, HEAD), HEAD)

    def pass_on(half, g):
        for c in (4, 5):
            @pl.when(pg_from(c))
            def _():
                pg_copy(g, c, half)[0].wait_recv()
                mid[c - 4, g, half] += rb[c - 1, g, half].astype(jnp.float32)

            sb[c - 3, g, half] = mid[c - 4, g, half].astype(jnp.bfloat16)
            pg_send(g, c - 2, half)

    def settle(half, g):
        for c in (1, 2, 3):
            @pl.when(pg_from(c))
            def _():
                pg_copy(g, c, half)[0].wait_recv()
                own[g, half] += rb[c - 1, g, half].astype(jnp.float32)
        done = own[g, half].astype(jnp.bfloat16)
        dkv[half, :, group_cols(g)] = done
        if half == 1:
            dvall[g, i] = done
            for m in range(1, nxc):
                ag_copy(g, m).start()

    def rs_copy(g, m):
        to = wrap(s + m)
        return remote(st1.at[g, to], r1.at[g, m - 1], rs_ss.at[g, m - 1], rs_rs.at[g, m - 1], seq=to)

    def weight(g):
        for m in range(1, nxc):
            src = dvall.at[g, lax.rem(i - m + nxc, nxc)]
            remote(src, src, ag_ss.at[g, m - 1], ag_rs.at[g, m - 1], dp=zh * nxc + lax.rem(i + m, nxc)).wait_recv()
        values = dvall[g].reshape(nxc * TOK, HEAD)
        product = jnp.dot(xp[...], values, preferred_element_type=jnp.float32)
        wf[g] = product
        st1[g] = product.astype(jnp.bfloat16).reshape(ns, part, HEAD)
        for m in range(1, ns):
            rs_copy(g, m).start()

    def z_copy(g, m):
        to = lax.rem(zh + m, nz)
        return remote(
            st2.at[g, to], r2.at[g, m - 1], z_ss.at[g, m - 1], z_rs.at[g, m - 1], dp=to * nxc + i
        )

    def sum_seq(g):
        mine = wf[g, pl.ds(pl.multiple_of(s * part, part), part), :]
        for m in range(1, ns):
            rs_copy(g, m).wait_recv()
            mine = mine + r1[g, m - 1].astype(jnp.float32)
        acc[g] = mine
        for n in range(nz):
            st2[g, n, :own_rows, :] = acc[g, n * own_rows:(n + 1) * own_rows, :]
        for m in range(1, nz):
            z_copy(g, m).start()

    def sum_z(g):
        result = st2[g, zh, :own_rows, :]
        for m in range(1, nz):
            z_copy(g, m).wait_recv()
            result = result + r2[g, m - 1, :own_rows, :]
        out_s[:, group_cols(g)] = result * ((ns * nz * nxc * TOK) ** -0.5)

    out_k = pltpu.make_async_copy(dkv.at[0], dk_hbm, out_sem.at[KV])
    out_v = pltpu.make_async_copy(dkv.at[1], dv_hbm, out_sem.at[KV + 1])
    out_w = pltpu.make_async_copy(out_s, dw_hbm, out_sem.at[KV + 2])

    stages = (
        (attend_values, 0),
        (functools.partial(forward, 1), 0),
        (functools.partial(pass_on, 1), 1),
        (functools.partial(settle, 1), 2),
        (weight, 3),
        (sum_seq, 4),
        (attend_keys, 2),
        (functools.partial(pass_on, 0), 3),
        (functools.partial(settle, 0), 4),
    )

    def step(t, carry):
        @pl.when(t == 2)
        def _():
            reorder_columns()

        for stage, behind in stages:
            @pl.when((t >= behind) & (t < behind + KV))
            def _():
                stage(t - behind)
        return carry

    lax.fori_loop(0, KV + max(behind for _, behind in stages), step, 0)
    out_k.start()
    out_v.start()
    for g in range(KV):
        sum_z(g)
    out_w.start()

    def drain(g, carry):
        for half in range(2):
            for n in range(6):
                copy, wanted = kv_copy(g, n, half)

                @pl.when(wanted)
                def _():
                    copy.wait_send()
            for c in range(1, len(REL)):
                sent, given = pg_copy(g, c, half)

                @pl.when(given)
                def _():
                    sent.wait_send()
        for m in range(1, nxc):
            ag_copy(g, m).wait_send()
        for m in range(1, ns):
            rs_copy(g, m).wait_send()
        for m in range(1, nz):
            z_copy(g, m).wait_send()
        dq_copy(g).wait()
        return carry

    lax.fori_loop(0, KV, drain, 0)
    for m in range(1, nxc):
        x_copy(m).wait_send()
    out_k.wait()
    out_v.wait()
    out_w.wait()


def finish(*refs):
    ins, outs, held, ld, out_sem = refs[:4], refs[4:8], refs[8:12], refs[12], refs[13]
    loads, stores = [], []
    for src, dst, mid in zip(ins, outs, held):
        for col in range(0, src.shape[1], KV * HEAD):
            n, part = len(loads), (slice(None), pl.ds(col, KV * HEAD))
            loads.append(pltpu.make_async_copy(src.at[part], mid.at[part], ld.at[n]))
            stores.append(pltpu.make_async_copy(mid.at[part], dst.at[part], out_sem.at[n]))
    for copy in loads:
        copy.start()
    for copy, store in zip(loads, stores):
        copy.wait()
        store.start()
    for store in stores:
        store.wait()


def solution(mesh, nx=4):
    ns = mesh.shape["seq"]
    nxc = nx * CORES
    nz = mesh.shape["dp"] // nxc

    def on_device(q, k, v, o, do, lse, x, docs, tiles):
        width = x.shape[2]
        own_rows = width // (ns * nz * nxc)
        part = own_rows * nz
        rows = part * ns
        padded = -(-own_rows // 8) * 8
        slots = len(REL)
        bf, f32 = jnp.bfloat16, jnp.float32
        hbm = pl.BlockSpec(memory_space=pl.ANY)
        smem = pl.BlockSpec(memory_space=pltpu.SMEM)
        dma = pltpu.SemaphoreType.DMA
        scratch = [
            pltpu.VMEM((TOK, HQ * HEAD), bf),
            pltpu.VMEM((TOK, HQ * HEAD), bf),
            pltpu.VMEM((TOK, HQ * HEAD), bf),
                        pltpu.VMEM((TOK, width), bf),
            pltpu.VMEM((slots, KV, 2, TOK, HEAD), bf),
            pltpu.VMEM((slots // 2, 2 * TOK, 2 * TOK), f32),
            pltpu.VMEM((HQ, TOK), f32),
            pltpu.VMEM((HQ, TOK), f32),
            pltpu.VMEM((KV, slots // 2, 2 * TOK, GROUP * TOK), f32),
            pltpu.VMEM((TOK, HQ * HEAD), bf),
            pltpu.VMEM((KV, 2, TOK, HEAD), f32),
            pltpu.VMEM((2, KV, 2, TOK, HEAD), f32),
            pltpu.VMEM((slots - 1, KV, 2, TOK, HEAD), bf),
            pltpu.VMEM((slots - 1, KV, 2, TOK, HEAD), bf),
            pltpu.VMEM((2, TOK, KV * HEAD), bf),
            pltpu.VMEM((nz, nxc, rows // nz, TOK), bf),
            pltpu.VMEM((nxc, nz, rows // nz, TOK), bf),
            pltpu.VMEM((rows, nxc * TOK), bf),
            pltpu.VMEM((KV, nxc, TOK, HEAD), bf),
            pltpu.VMEM((KV, rows, HEAD), f32),
            pltpu.VMEM((KV, ns, part, HEAD), bf),
            pltpu.VMEM((KV, ns - 1, part, HEAD), bf),
            pltpu.VMEM((KV, part, HEAD), f32),
            pltpu.VMEM((KV, nz, padded, HEAD), f32),
            pltpu.VMEM((KV, max(nz - 1, 1), padded, HEAD), f32),
            pltpu.VMEM((own_rows, KV * HEAD), f32),
            dma((KV, 2)),
            dma((5,)),
            dma((KV + 3,)),
            dma((slots, KV, 2)),
            dma((slots - 1, KV, 2)),
            dma((slots - 1, KV, 2)),
            dma((slots - 1, KV, 2)),
            dma((nxc - 1,)),
            dma((nxc - 1,)),
            dma((KV, nxc - 1)),
            dma((KV, nxc - 1)),
            dma((KV, ns - 1)),
            dma((KV, ns - 1)),
            dma((KV, max(nz - 1, 1))),
            dma((KV, max(nz - 1, 1))),
        ]
        shapes = (
            jax.ShapeDtypeStruct((TOK, HQ * HEAD), bf),
            jax.ShapeDtypeStruct((TOK, KV * HEAD), bf),
            jax.ShapeDtypeStruct((TOK, KV * HEAD), bf),
            jax.ShapeDtypeStruct((own_rows, KV * HEAD), f32),
        )
        results = pl.pallas_call(
            functools.partial(kernel, nx, nz, ns),
            out_shape=shapes,
            in_specs=[smem, smem] + [hbm] * 7,
            out_specs=(hbm,) * 4,
            scratch_shapes=scratch,
            compiler_params=pltpu.CompilerParams(
                collective_id=0, has_side_effects=True, vmem_limit_bytes=60 * 2**20
            ),
        )(docs, tiles, q[0], k[0], v[0], o[0], do[0], lse[0].T, x[0])
        dq, dk, dv, dw = pl.pallas_call(
            finish,
            out_shape=shapes,
            in_specs=[hbm] * 4,
            out_specs=(hbm,) * 4,
            scratch_shapes=[pltpu.VMEM(a.shape, a.dtype) for a in shapes] + [dma((GROUP + 3,))] * 2,
            compiler_params=pltpu.CompilerParams(vmem_limit_bytes=60 * 2**20),
        )(*results)
        return dq[None], dk[None], dv[None], dw

    split = P("dp", "seq", None)
    return jax.shard_map(
        on_device,
        mesh=mesh,
        in_specs=(split,) * 7 + (P("dp", None),) * 2,
        out_specs=(split,) * 3 + (P(("dp", "seq"), None),),
        check_vma=False,
    )
```

```python
import functools
import math

import jax
import jax.numpy as jnp
from jax import lax
from jax.experimental import pallas as pl
from jax.experimental.pallas import tpu as pltpu
from jax.sharding import PartitionSpec as P

HQ = 32
KV = 4
HEAD = 128
GROUP = HQ // KV
TILE_TOK = 32
TOK = 128
CORES = 2
SCALE = HEAD ** -0.5
LOG2E = math.log2(math.e)
HIDDEN = -1e30
REL = (0, 1, -1, -2, -3, -4)
NT = (((1,), (1,)), ((), ()))


def kernel(
    nx, nz, ns, doc_ref, tiles_ref, q_hbm, k_hbm, v_hbm, o_hbm, do_hbm, lse_hbm, x_hbm,
    dq_hbm, dk_hbm, dv_hbm, dw_hbm,
    q_s, o_s, do_s, x_s, kvb, bias, lse_t, delta_s, prob_s, dq_s, own, mid, sb, rb, dkv,
    x_t, xg, xp, dvall, wf, st1, r1, acc, st2, r2, out_s,
    ld_kv, ld, out_sem, kv_ss, kv_rs, pg_ss, pg_rs, x_ss, x_rs, ag_ss, ag_rs, rs_ss, rs_rs, z_ss, z_rs,
):
    nxc = nx * CORES
    d = lax.axis_index("dp")
    s = lax.axis_index("seq")
    zh = d // nxc
    i = lax.rem(d, nxc)
    xc = i // CORES
    core = lax.rem(i, CORES)
    rows = wf.shape[1]
    part = rows // ns
    own_rows = part // nz

    def remote(src, dst, ss, rs, **where):
        return pltpu.make_async_remote_copy(
            src_ref=src, dst_ref=dst, send_sem=ss, recv_sem=rs, device_id=where,
            device_id_type=pl.DeviceIdType.MESH,
        )

    def inside(t):
        return (t >= 0) & (t < ns)

    def wrap(t):
        return lax.rem(t + ns, ns)

    barrier = pltpu.get_barrier_semaphore()
    peers = [dict(seq=wrap(s + m)) for m in range(1, ns)]
    peers += [dict(dp=zh * nxc + lax.rem(i + m, nxc)) for m in range(1, nxc)]
    peers += [dict(dp=lax.rem(zh + m, nz) * nxc + i) for m in range(1, nz)]
    for peer in peers:
        pl.semaphore_signal(barrier, inc=1, device_id=peer, device_id_type=pl.DeviceIdType.MESH)

    def kv_load(g, half):
        src = (k_hbm, v_hbm)[half]
        return pltpu.make_async_copy(src.at[:, pl.ds(g * HEAD, HEAD)], kvb.at[0, g, half], ld_kv.at[g, half])

    for g in range(KV):
        kv_load(g, 0).start()
        kv_load(g, 1).start()
    loads = [
        pltpu.make_async_copy(src, dst, ld.at[n])
        for n, (src, dst) in enumerate(
            ((x_hbm, x_s), (do_hbm, do_s), (o_hbm, o_s), (q_hbm, q_s), (lse_hbm, lse_t))
        )
    ]
    for copy in loads:
        copy.start()
    for c in range(1, len(REL)):
        @pl.when(jnp.logical_not(inside(s + REL[c])))
        def _():
            kvb[c] = jnp.zeros(kvb.shape[1:], kvb.dtype)
    st2[...] = jnp.zeros(st2.shape, st2.dtype)

    z = lax.rem(s, 2)

    def kv_copy(g, n, half):
        held, slot, to, wanted = (
            (0, 2 - z, s + 1 - 2 * z, True),
            (0, 3, s + 2, True),
            (3, 5, s + 2, inside(s - 2)),
            (1 + z, 2 + 2 * z, s + 2, True),
            (2, 1, s - 2, z == 1),
            (5, 4, s - 1, (z == 1) & inside(s - 4)),
        )[n]
        copy = remote(
            kvb.at[held, g, half], kvb.at[slot, g, half], kv_ss.at[n, g, half], kv_rs.at[slot - 1, g, half],
            seq=wrap(to),
        )
        return copy, inside(to) & wanted

    def kv_send(g, n, half):
        copy, wanted = kv_copy(g, n, half)

        @pl.when(wanted)
        def _():
            copy.start()

    def kv_arrived(g, c, half):
        remote(
            kvb.at[0, g, half], kvb.at[c, g, half], kv_ss.at[0, g, half], kv_rs.at[c - 1, g, half],
            seq=wrap(s + 1),
        ).wait_recv()

    def pg_copy(g, c, half):
        to = s - 2 if c >= 4 and half == 0 else s + REL[c]
        copy = remote(
            sb.at[c - 1, g, half], rb.at[c - 1, g, half], pg_ss.at[c - 1, g, half], pg_rs.at[c - 1, g, half],
            seq=wrap(to),
        )
        return copy, inside(s + REL[c])

    def pg_send(g, c, half):
        copy, wanted = pg_copy(g, c, half)

        @pl.when(wanted)
        def _():
            copy.start()

    def pg_from(c, half):
        return inside(s + 2) & inside(s + 2 + REL[c]) if c >= 4 and half == 0 else inside(s - REL[c])

    loads[0].wait()
    slab = rows // nz
    for tile in range(x_s.shape[1] // TOK):
        turned = x_s[:, tile * TOK:(tile + 1) * TOK].T
        at = tile * TOK
        while at < (tile + 1) * TOK:
            block, offset = divmod(at, slab)
            length = min((tile + 1) * TOK - at, slab - offset)
            lead = at - tile * TOK
            x_t[block // nxc, block % nxc, offset:offset + length, :] = turned[lead:lead + length, :]
            at += length

    def x_copy(m):
        j = lax.rem(i + m, nxc)
        return remote(x_t.at[:, j], xg.at[i], x_ss.at[m - 1], x_rs.at[m - 1], dp=zh * nxc + j)

    xg[i] = x_t[:, i]

    row = s * TOK + lax.broadcasted_iota(jnp.int32, (1, TOK), 1)
    low = jnp.zeros((1, TOK), jnp.int32)
    high = jnp.zeros((1, TOK), jnp.int32)
    start = jnp.int32(0)
    for n in range(doc_ref.shape[1]):
        length = doc_ref[0, n]
        image_end = start + jnp.minimum(tiles_ref[0, n] * TILE_TOK, length)
        here = row >= start
        low = jnp.where(here, start, low)
        high = jnp.where(here, image_end, high)
        start = start + length
    high = jnp.maximum(row + 1, high)
    for c in range(len(REL)):
        key = (s + REL[c]) * TOK + lax.broadcasted_iota(jnp.int32, (TOK, TOK), 0)
        tile = jnp.where((key >= low) & (key < high), 0.0, HIDDEN).astype(jnp.float32)
        p, half = divmod(c, 2)
        bias[p, half * TOK:(half + 1) * TOK, :TOK] = tile
        bias[p, half * TOK:(half + 1) * TOK, TOK:] = tile
    for g in range(KV):
        kv_load(g, 0).wait()
        kv_load(g, 1).wait()
    pl.semaphore_wait(barrier, len(peers))
    def send_own(half):
        for g in range(KV):
            kv_send(g, 0, half)
            kv_send(g, 1, half)

    send_own(0)
    for m in range(1, nxc):
        x_copy(m).start()
    for copy in loads[1:]:
        copy.wait()

    head_lane = lax.broadcasted_iota(jnp.int32, (GROUP, GROUP * HEAD), 1)
    head_row = lax.broadcasted_iota(jnp.int32, (GROUP, GROUP * HEAD), 0)
    picks = ((head_lane >= head_row * HEAD) & (head_lane < (head_row + 1) * HEAD)).astype(jnp.bfloat16)

    def dq_copy(g):
        cols = pl.ds(g * GROUP * HEAD, GROUP * HEAD)
        return pltpu.make_async_copy(dq_s.at[:, cols], dq_hbm.at[:, cols], out_sem.at[g])

    def group_rows(g):
        return pl.ds(pl.multiple_of(g * GROUP, GROUP), GROUP)

    def row_delta(g, carry):
        wide = pl.ds(pl.multiple_of(g * GROUP * HEAD, GROUP * HEAD), GROUP * HEAD)
        product = do_s[:, wide].astype(jnp.float32) * o_s[:, wide].astype(jnp.float32)
        coarse = product.astype(jnp.bfloat16)
        fine = (product - coarse.astype(jnp.float32)).astype(jnp.bfloat16)
        delta = lax.dot_general(picks, coarse, NT, preferred_element_type=jnp.float32)
        delta += lax.dot_general(picks, fine, NT, preferred_element_type=jnp.float32)
        delta_s[group_rows(g), :] = delta
        return carry

    def forward(half, g):
        @pl.when(z == 0)
        def _():
            kv_arrived(g, 1, half)

        @pl.when(z == 1)
        def _():
            kv_arrived(g, 2, half)

        kv_send(g, 3, half)
        kv_send(g, 4, half)

        @pl.when(inside(s - 2))
        def _():
            kv_arrived(g, 3, half)

        kv_send(g, 2, half)

    def forward_keys(g, carry):
        forward(0, g)
        return carry

    lax.fori_loop(0, KV, forward_keys, 0)
    send_own(1)

    def heads(ref, g):
        return jnp.concatenate([ref[:, pl.ds((g * GROUP + h) * HEAD, HEAD)] for h in range(GROUP)], axis=0)

    def await_blocks(g, p, half):
        awaited = (
            ((1, z == 1),),
            ((5, z == 1), (2, z == 0)),
            ((4, z >= 0), (5, z == 0)),
        )[p]
        for c, here in awaited:
            @pl.when(inside(s + REL[c]) & here)
            def _():
                kv_arrived(g, c, half)

            if p == 1 and c == 5:
                kv_send(g, 5, half)
        return jnp.concatenate([kvb[2 * p, g, half], kvb[2 * p + 1, g, half]], axis=0)

    def keep(g, p, half, partial):
        for c in (2 * p, 2 * p + 1):
            block = partial[(c - 2 * p) * TOK:(c - 2 * p + 1) * TOK]
            if c == 0:
                own[g, half] = block
            elif c in (2, 3) and half == 0:
                mid[c - 2, g] = block
            else:
                sb[c - 1, g, half] = block.astype(jnp.bfloat16)
                pg_send(g, c, half)

    pairs = [(n, slice(n * 2 * TOK, (n + 1) * 2 * TOK)) for n in range(GROUP // 2)]

    def two_rows(stat, n):
        return jnp.concatenate([stat[2 * n:2 * n + 1], stat[2 * n + 1:2 * n + 2]], axis=1)

    def attend_values(g):
        stat = lse_t[group_rows(g), :] * LOG2E
        q8, do8 = heads(q_s, g), heads(do_s, g)
        for p in range(len(REL) // 2):
            keys = await_blocks(g, p, 0)
            probs = []
            for n, cut in pairs:
                scores = lax.dot_general(keys, q8[cut], NT, preferred_element_type=jnp.float32)
                prob = jnp.exp2(scores * (SCALE * LOG2E) - two_rows(stat, n) + bias[p])
                prob_s[g, p, :, cut] = prob
                probs.append(prob.astype(jnp.bfloat16))
            probs = jnp.concatenate(probs, axis=1)
            keep(g, p, 1, jnp.dot(probs, do8, preferred_element_type=jnp.float32))

    def attend_keys(g):
        delta = delta_s[group_rows(g), :]
        q8, do8 = heads(q_s, g), heads(do_s, g)
        total = None
        for p in range(len(REL) // 2):
            values = await_blocks(g, p, 1)
            keys = jnp.concatenate([kvb[2 * p, g, 0], kvb[2 * p + 1, g, 0]], axis=0)
            steps = []
            for n, cut in pairs:
                grad = lax.dot_general(values, do8[cut], NT, preferred_element_type=jnp.float32)
                steps.append((prob_s[g, p, :, cut] * (grad - two_rows(delta, n))).astype(jnp.bfloat16))
            steps = jnp.concatenate(steps, axis=1)
            keep(g, p, 0, jnp.dot(steps, q8, preferred_element_type=jnp.float32) * SCALE)
            dq = jnp.dot(keys.T, steps, preferred_element_type=jnp.float32)
            total = dq if total is None else total + dq
        for h in range(GROUP):
            dq_s[:, pl.ds((g * GROUP + h) * HEAD, HEAD)] = (
                total[:, h * TOK:(h + 1) * TOK].T * SCALE
            ).astype(jnp.bfloat16)
        dq_copy(g).start()

    def reorder_columns():
        old = lax.broadcasted_iota(jnp.int32, (1, rows), 1)
        new = old
        before = 0
        for n in range(1, nz * ns):
            shift = (n % ns * nz + n // ns - n) * own_rows
            new = new + jnp.where(old >= n * own_rows, shift - before, 0)
            before = shift
        order = (lax.broadcasted_iota(jnp.int32, (rows, rows), 0) == new).astype(jnp.bfloat16)
        for m in range(1, nxc):
            x_copy(m).wait_recv()

        def reorder(jj, carry):
            two = jnp.concatenate([xg[2 * jj].reshape(rows, TOK), xg[2 * jj + 1].reshape(rows, TOK)], axis=1)
            xp[:, pl.ds(pl.multiple_of(jj * 2 * TOK, 2 * TOK), 2 * TOK)] = jnp.dot(
                order, two, preferred_element_type=jnp.float32
            ).astype(jnp.bfloat16)
            return carry

        lax.fori_loop(0, nxc // 2, reorder, 0)

    def ag_copy(g, m):
        to = lax.rem(i + m, nxc)
        return remote(
            dvall.at[g, i], dvall.at[g, i], ag_ss.at[g, m - 1], ag_rs.at[g, m - 1], dp=zh * nxc + to
        )

    def group_cols(g):
        return pl.ds(pl.multiple_of(g * HEAD, HEAD), HEAD)

    def pass_on(g):
        for c in (4, 5):
            @pl.when(pg_from(c, 0))
            def _():
                pg_copy(g, c, 0)[0].wait_recv()
                mid[c - 4, g] += rb[c - 1, g, 0].astype(jnp.float32)

            sb[c - 3, g, 0] = mid[c - 4, g].astype(jnp.bfloat16)
            pg_send(g, c - 2, 0)

    def settle(half, g):
        for c in (1, 2, 3) if half == 0 else range(1, len(REL)):
            @pl.when(pg_from(c, half))
            def _():
                pg_copy(g, c, half)[0].wait_recv()
                own[g, half] += rb[c - 1, g, half].astype(jnp.float32)
        done = own[g, half].astype(jnp.bfloat16)
        dkv[half, :, group_cols(g)] = done
        if half == 1:
            dvall[g, i] = done
            for m in range(1, nxc):
                ag_copy(g, m).start()

    def rs_copy(g, m):
        to = wrap(s + m)
        return remote(st1.at[g, to], r1.at[g, m - 1], rs_ss.at[g, m - 1], rs_rs.at[g, m - 1], seq=to)

    def weight(g):
        @pl.when(g == 0)
        def _():
            reorder_columns()

        for m in range(1, nxc):
            src = dvall.at[g, lax.rem(i - m + nxc, nxc)]
            remote(src, src, ag_ss.at[g, m - 1], ag_rs.at[g, m - 1], dp=zh * nxc + lax.rem(i + m, nxc)).wait_recv()
        values = dvall[g].reshape(nxc * TOK, HEAD)
        product = jnp.dot(xp[...], values, preferred_element_type=jnp.float32)
        wf[g] = product
        st1[g] = product.astype(jnp.bfloat16).reshape(ns, part, HEAD)
        for m in range(1, ns):
            rs_copy(g, m).start()

    def z_copy(g, m):
        to = lax.rem(zh + m, nz)
        return remote(
            st2.at[g, to], r2.at[g, m - 1], z_ss.at[g, m - 1], z_rs.at[g, m - 1], dp=to * nxc + i
        )

    def sum_seq(g):
        mine = wf[g, pl.ds(pl.multiple_of(s * part, part), part), :]
        for m in range(1, ns):
            rs_copy(g, m).wait_recv()
            mine = mine + r1[g, m - 1].astype(jnp.float32)
        acc[g] = mine
        for n in range(nz):
            st2[g, n, :own_rows, :] = acc[g, n * own_rows:(n + 1) * own_rows, :]
        for m in range(1, nz):
            z_copy(g, m).start()

    def sum_z(g):
        result = st2[g, zh, :own_rows, :]
        for m in range(1, nz):
            z_copy(g, m).wait_recv()
            result = result + r2[g, m - 1, :own_rows, :]
        out_s[:, group_cols(g)] = result * ((ns * nz * nxc * TOK) ** -0.5)

    out_k = pltpu.make_async_copy(dkv.at[0], dk_hbm, out_sem.at[KV])
    out_v = pltpu.make_async_copy(dkv.at[1], dv_hbm, out_sem.at[KV + 1])
    out_w = pltpu.make_async_copy(out_s, dw_hbm, out_sem.at[KV + 2])

    stages = (
        (attend_values, 0),
        (functools.partial(settle, 1), 1),
        (functools.partial(forward, 1), 1),
        (weight, 2),
        (sum_seq, 3),
        (attend_keys, 2),
        (pass_on, 3),
        (functools.partial(settle, 0), 4),
    )

    def step(t, carry):
        @pl.when(t == 1)
        def _():
            lax.fori_loop(0, KV, row_delta, 0)

        for stage, behind in stages:
            @pl.when((t >= behind) & (t < behind + KV))
            def _():
                stage(t - behind)
        return carry

    lax.fori_loop(0, KV + max(behind for _, behind in stages), step, 0)
    out_k.start()
    out_v.start()
    for g in range(KV):
        sum_z(g)
    out_w.start()

    def drain(g, carry):
        for half in range(2):
            for n in range(6):
                copy, wanted = kv_copy(g, n, half)

                @pl.when(wanted)
                def _():
                    copy.wait_send()
            for c in range(1, len(REL)):
                sent, given = pg_copy(g, c, half)

                @pl.when(given)
                def _():
                    sent.wait_send()
        for m in range(1, nxc):
            ag_copy(g, m).wait_send()
        for m in range(1, ns):
            rs_copy(g, m).wait_send()
        for m in range(1, nz):
            z_copy(g, m).wait_send()
        dq_copy(g).wait()
        return carry

    lax.fori_loop(0, KV, drain, 0)
    for m in range(1, nxc):
        x_copy(m).wait_send()
    out_k.wait()
    out_v.wait()
    out_w.wait()


def finish(*refs):
    ins, outs, held, ld, out_sem = refs[:4], refs[4:8], refs[8:12], refs[12], refs[13]
    loads, stores = [], []
    for src, dst, mid in zip(ins, outs, held):
        for col in range(0, src.shape[1], KV * HEAD):
            n, part = len(loads), (slice(None), pl.ds(col, KV * HEAD))
            loads.append(pltpu.make_async_copy(src.at[part], mid.at[part], ld.at[n]))
            stores.append(pltpu.make_async_copy(mid.at[part], dst.at[part], out_sem.at[n]))
    for copy in loads:
        copy.start()
    for copy, store in zip(loads, stores):
        copy.wait()
        store.start()
    for store in stores:
        store.wait()


def solution(mesh, nx=4):
    ns = mesh.shape["seq"]
    nxc = nx * CORES
    nz = mesh.shape["dp"] // nxc

    def on_device(q, k, v, o, do, lse, x, docs, tiles):
        width = x.shape[2]
        own_rows = width // (ns * nz * nxc)
        part = own_rows * nz
        rows = part * ns
        padded = -(-own_rows // 8) * 8
        slots = len(REL)
        bf, f32 = jnp.bfloat16, jnp.float32
        hbm = pl.BlockSpec(memory_space=pl.ANY)
        smem = pl.BlockSpec(memory_space=pltpu.SMEM)
        dma = pltpu.SemaphoreType.DMA
        scratch = [
            pltpu.VMEM((TOK, HQ * HEAD), bf),
            pltpu.VMEM((TOK, HQ * HEAD), bf),
            pltpu.VMEM((TOK, HQ * HEAD), bf),
                        pltpu.VMEM((TOK, width), bf),
            pltpu.VMEM((slots, KV, 2, TOK, HEAD), bf),
            pltpu.VMEM((slots // 2, 2 * TOK, 2 * TOK), f32),
            pltpu.VMEM((HQ, TOK), f32),
            pltpu.VMEM((HQ, TOK), f32),
            pltpu.VMEM((KV, slots // 2, 2 * TOK, GROUP * TOK), f32),
            pltpu.VMEM((TOK, HQ * HEAD), bf),
            pltpu.VMEM((KV, 2, TOK, HEAD), f32),
            pltpu.VMEM((2, KV, TOK, HEAD), f32),
            pltpu.VMEM((slots - 1, KV, 2, TOK, HEAD), bf),
            pltpu.VMEM((slots - 1, KV, 2, TOK, HEAD), bf),
            pltpu.VMEM((2, TOK, KV * HEAD), bf),
            pltpu.VMEM((nz, nxc, rows // nz, TOK), bf),
            pltpu.VMEM((nxc, nz, rows // nz, TOK), bf),
            pltpu.VMEM((rows, nxc * TOK), bf),
            pltpu.VMEM((KV, nxc, TOK, HEAD), bf),
            pltpu.VMEM((KV, rows, HEAD), f32),
            pltpu.VMEM((KV, ns, part, HEAD), bf),
            pltpu.VMEM((KV, ns - 1, part, HEAD), bf),
            pltpu.VMEM((KV, part, HEAD), f32),
            pltpu.VMEM((KV, nz, padded, HEAD), f32),
            pltpu.VMEM((KV, max(nz - 1, 1), padded, HEAD), f32),
            pltpu.VMEM((own_rows, KV * HEAD), f32),
            dma((KV, 2)),
            dma((5,)),
            dma((KV + 3,)),
            dma((slots, KV, 2)),
            dma((slots - 1, KV, 2)),
            dma((slots - 1, KV, 2)),
            dma((slots - 1, KV, 2)),
            dma((nxc - 1,)),
            dma((nxc - 1,)),
            dma((KV, nxc - 1)),
            dma((KV, nxc - 1)),
            dma((KV, ns - 1)),
            dma((KV, ns - 1)),
            dma((KV, max(nz - 1, 1))),
            dma((KV, max(nz - 1, 1))),
        ]
        shapes = (
            jax.ShapeDtypeStruct((TOK, HQ * HEAD), bf),
            jax.ShapeDtypeStruct((TOK, KV * HEAD), bf),
            jax.ShapeDtypeStruct((TOK, KV * HEAD), bf),
            jax.ShapeDtypeStruct((own_rows, KV * HEAD), f32),
        )
        results = pl.pallas_call(
            functools.partial(kernel, nx, nz, ns),
            out_shape=shapes,
            in_specs=[smem, smem] + [hbm] * 7,
            out_specs=(hbm,) * 4,
            scratch_shapes=scratch,
            compiler_params=pltpu.CompilerParams(
                collective_id=0, has_side_effects=True, vmem_limit_bytes=60 * 2**20
            ),
        )(docs, tiles, q[0], k[0], v[0], o[0], do[0], lse[0].T, x[0])
        dq, dk, dv, dw = pl.pallas_call(
            finish,
            out_shape=shapes,
            in_specs=[hbm] * 4,
            out_specs=(hbm,) * 4,
            scratch_shapes=[pltpu.VMEM(a.shape, a.dtype) for a in shapes] + [dma((GROUP + 3,))] * 2,
            compiler_params=pltpu.CompilerParams(vmem_limit_bytes=60 * 2**20),
        )(*results)
        return dq[None], dk[None], dv[None], dw

    split = P("dp", "seq", None)
    return jax.shard_map(
        on_device,
        mesh=mesh,
        in_specs=(split,) * 7 + (P("dp", None),) * 2,
        out_specs=(split,) * 3 + (P(("dp", "seq"), None),),
        check_vma=False,
    )
```

```python
import functools
import math

import jax
import jax.numpy as jnp
from jax import lax
from jax.experimental import pallas as pl
from jax.experimental.pallas import tpu as pltpu
from jax.sharding import PartitionSpec as P

HQ = 32
KV = 4
HEAD = 128
GROUP = HQ // KV
TILE_TOK = 32
TOK = 128
CORES = 2
SCALE = HEAD ** -0.5
LOG2E = math.log2(math.e)
HIDDEN = -1e30
REL = (0, 1, -1, -2, -3, -4)
NT = (((1,), (1,)), ((), ()))


def far_first(n):
    return sorted(range(1, n), key=lambda m: abs(2 * m - n))


def kernel(
    nx, nz, ns, doc_ref, tiles_ref, q_hbm, k_hbm, v_hbm, o_hbm, do_hbm, lse_hbm, x_hbm,
    dq_hbm, dk_hbm, dv_hbm, dw_hbm,
    q_s, o_s, do_s, x_s, kvb, bias, lse_t, delta_s, prob_s, dq_s, own, mid, sb, rb, dkv,
    x_t, xg, xp, dvall, wf, st1, r1, acc, st2, r2, out_s,
    ld_kv, ld, out_sem, kv_ss, kv_rs, pg_ss, pg_rs, x_ss, x_rs, ag_ss, ag_rs, rs_ss, rs_rs, z_ss, z_rs,
):
    nxc = nx * CORES
    d = lax.axis_index("dp")
    s = lax.axis_index("seq")
    zh = d // nxc
    i = lax.rem(d, nxc)
    xc = i // CORES
    core = lax.rem(i, CORES)
    rows = wf.shape[1]
    part = rows // ns
    own_rows = part // nz

    def remote(src, dst, ss, rs, **where):
        return pltpu.make_async_remote_copy(
            src_ref=src, dst_ref=dst, send_sem=ss, recv_sem=rs, device_id=where,
            device_id_type=pl.DeviceIdType.MESH,
        )

    def inside(t):
        return (t >= 0) & (t < ns)

    def wrap(t):
        return lax.rem(t + ns, ns)

    barrier = pltpu.get_barrier_semaphore()
    peers = [dict(seq=wrap(s + m)) for m in range(1, ns)]
    peers += [dict(dp=zh * nxc + lax.rem(i + m, nxc)) for m in range(1, nxc)]
    peers += [dict(dp=lax.rem(zh + m, nz) * nxc + i) for m in range(1, nz)]
    for peer in peers:
        pl.semaphore_signal(barrier, inc=1, device_id=peer, device_id_type=pl.DeviceIdType.MESH)

    def kv_load(g, half):
        src = (k_hbm, v_hbm)[half]
        return pltpu.make_async_copy(src.at[:, pl.ds(g * HEAD, HEAD)], kvb.at[0, g, half], ld_kv.at[g, half])

    for g in range(KV):
        kv_load(g, 0).start()
        kv_load(g, 1).start()
    loads = [
        pltpu.make_async_copy(src, dst, ld.at[n])
        for n, (src, dst) in enumerate(
            ((x_hbm, x_s), (do_hbm, do_s), (o_hbm, o_s), (q_hbm, q_s), (lse_hbm, lse_t))
        )
    ]
    for copy in loads:
        copy.start()
    for c in range(1, len(REL)):
        @pl.when(jnp.logical_not(inside(s + REL[c])))
        def _():
            kvb[c] = jnp.zeros(kvb.shape[1:], kvb.dtype)
    st2[...] = jnp.zeros(st2.shape, st2.dtype)

    z = lax.rem(s, 2)

    def kv_copy(g, n, half):
        held, slot, to, wanted = (
            (0, 2 - z, s + 1 - 2 * z, True),
            (0, 3, s + 2, True),
            (3, 5, s + 2, inside(s - 2)),
            (1 + z, 2 + 2 * z, s + 2, True),
            (2, 1, s - 2, z == 1),
            (5, 4, s - 1, (z == 1) & inside(s - 4)),
        )[n]
        copy = remote(
            kvb.at[held, g, half], kvb.at[slot, g, half], kv_ss.at[n, g, half], kv_rs.at[slot - 1, g, half],
            seq=wrap(to),
        )
        return copy, inside(to) & wanted

    def kv_send(g, n, half):
        copy, wanted = kv_copy(g, n, half)

        @pl.when(wanted)
        def _():
            copy.start()

    def kv_arrived(g, c, half):
        remote(
            kvb.at[0, g, half], kvb.at[c, g, half], kv_ss.at[0, g, half], kv_rs.at[c - 1, g, half],
            seq=wrap(s + 1),
        ).wait_recv()

    def pg_copy(g, c, half):
        to = s - 2 if c >= 4 and half == 0 else s + REL[c]
        copy = remote(
            sb.at[c - 1, g, half], rb.at[c - 1, g, half], pg_ss.at[c - 1, g, half], pg_rs.at[c - 1, g, half],
            seq=wrap(to),
        )
        return copy, inside(s + REL[c])

    def pg_send(g, c, half):
        copy, wanted = pg_copy(g, c, half)

        @pl.when(wanted)
        def _():
            copy.start()

    def pg_from(c, half):
        return inside(s + 2) & inside(s + 2 + REL[c]) if c >= 4 and half == 0 else inside(s - REL[c])

    loads[0].wait()
    slab = rows // nz
    for tile in range(x_s.shape[1] // TOK):
        turned = x_s[:, tile * TOK:(tile + 1) * TOK].T
        at = tile * TOK
        while at < (tile + 1) * TOK:
            block, offset = divmod(at, slab)
            length = min((tile + 1) * TOK - at, slab - offset)
            lead = at - tile * TOK
            x_t[block // nxc, block % nxc, offset:offset + length, :] = turned[lead:lead + length, :]
            at += length

    def x_copy(m):
        j = lax.rem(i + m, nxc)
        return remote(x_t.at[:, j], xg.at[i], x_ss.at[m - 1], x_rs.at[m - 1], dp=zh * nxc + j)

    xg[i] = x_t[:, i]

    row = s * TOK + lax.broadcasted_iota(jnp.int32, (1, TOK), 1)
    low = jnp.zeros((1, TOK), jnp.int32)
    high = jnp.zeros((1, TOK), jnp.int32)
    start = jnp.int32(0)
    for n in range(doc_ref.shape[1]):
        length = doc_ref[0, n]
        image_end = start + jnp.minimum(tiles_ref[0, n] * TILE_TOK, length)
        here = row >= start
        low = jnp.where(here, start, low)
        high = jnp.where(here, image_end, high)
        start = start + length
    high = jnp.maximum(row + 1, high)
    for c in range(len(REL)):
        key = (s + REL[c]) * TOK + lax.broadcasted_iota(jnp.int32, (TOK, TOK), 0)
        tile = jnp.where((key >= low) & (key < high), 0.0, HIDDEN).astype(jnp.float32)
        p, half = divmod(c, 2)
        bias[p, half * TOK:(half + 1) * TOK, :TOK] = tile
        bias[p, half * TOK:(half + 1) * TOK, TOK:] = tile
    for g in range(KV):
        kv_load(g, 0).wait()
        kv_load(g, 1).wait()
    pl.semaphore_wait(barrier, len(peers))
    def send_own(half):
        for g in range(KV):
            kv_send(g, 0, half)
            kv_send(g, 1, half)

    send_own(0)
    for m in far_first(nxc):
        x_copy(m).start()
    for copy in loads[1:]:
        copy.wait()

    head_lane = lax.broadcasted_iota(jnp.int32, (GROUP, GROUP * HEAD), 1)
    head_row = lax.broadcasted_iota(jnp.int32, (GROUP, GROUP * HEAD), 0)
    picks = ((head_lane >= head_row * HEAD) & (head_lane < (head_row + 1) * HEAD)).astype(jnp.bfloat16)

    def dq_copy(g):
        cols = pl.ds(g * GROUP * HEAD, GROUP * HEAD)
        return pltpu.make_async_copy(dq_s.at[:, cols], dq_hbm.at[:, cols], out_sem.at[g])

    def group_rows(g):
        return pl.ds(pl.multiple_of(g * GROUP, GROUP), GROUP)

    def row_delta(g, carry):
        wide = pl.ds(pl.multiple_of(g * GROUP * HEAD, GROUP * HEAD), GROUP * HEAD)
        product = do_s[:, wide].astype(jnp.float32) * o_s[:, wide].astype(jnp.float32)
        coarse = product.astype(jnp.bfloat16)
        fine = (product - coarse.astype(jnp.float32)).astype(jnp.bfloat16)
        delta = lax.dot_general(picks, coarse, NT, preferred_element_type=jnp.float32)
        delta += lax.dot_general(picks, fine, NT, preferred_element_type=jnp.float32)
        delta_s[group_rows(g), :] = delta
        return carry

    def forward(half, g):
        @pl.when(z == 0)
        def _():
            kv_arrived(g, 1, half)

        @pl.when(z == 1)
        def _():
            kv_arrived(g, 2, half)

        kv_send(g, 3, half)
        kv_send(g, 4, half)

        @pl.when(inside(s - 2))
        def _():
            kv_arrived(g, 3, half)

        kv_send(g, 2, half)

    def forward_keys(g, carry):
        forward(0, g)
        return carry

    lax.fori_loop(0, KV, forward_keys, 0)
    send_own(1)

    def heads(ref, g):
        return jnp.concatenate([ref[:, pl.ds((g * GROUP + h) * HEAD, HEAD)] for h in range(GROUP)], axis=0)

    def await_blocks(g, p, half):
        awaited = (
            ((1, z == 1),),
            ((5, z == 1), (2, z == 0)),
            ((4, z >= 0), (5, z == 0)),
        )[p]
        for c, here in awaited:
            @pl.when(inside(s + REL[c]) & here)
            def _():
                kv_arrived(g, c, half)

            if p == 1 and c == 5:
                kv_send(g, 5, half)
        return jnp.concatenate([kvb[2 * p, g, half], kvb[2 * p + 1, g, half]], axis=0)

    def keep(g, p, half, partial):
        for c in (2 * p, 2 * p + 1):
            block = partial[(c - 2 * p) * TOK:(c - 2 * p + 1) * TOK]
            if c == 0:
                own[g, half] = block
            elif c in (2, 3) and half == 0:
                mid[c - 2, g] = block
            else:
                sb[c - 1, g, half] = block.astype(jnp.bfloat16)
                pg_send(g, c, half)

    pairs = [(n, slice(n * 2 * TOK, (n + 1) * 2 * TOK)) for n in range(GROUP // 2)]

    def two_rows(stat, n):
        return jnp.concatenate([stat[2 * n:2 * n + 1], stat[2 * n + 1:2 * n + 2]], axis=1)

    def attend_values(g):
        stat = lse_t[group_rows(g), :] * LOG2E
        q8, do8 = heads(q_s, g), heads(do_s, g)
        for p in range(len(REL) // 2):
            keys = await_blocks(g, p, 0)
            probs = []
            for n, cut in pairs:
                scores = lax.dot_general(keys, q8[cut], NT, preferred_element_type=jnp.float32)
                prob = jnp.exp2(scores * (SCALE * LOG2E) - two_rows(stat, n) + bias[p])
                prob_s[g, p, :, cut] = prob
                probs.append(prob.astype(jnp.bfloat16))
            probs = jnp.concatenate(probs, axis=1)
            keep(g, p, 1, jnp.dot(probs, do8, preferred_element_type=jnp.float32))

    def attend_keys(g):
        delta = delta_s[group_rows(g), :]
        q8, do8 = heads(q_s, g), heads(do_s, g)
        total = None
        for p in range(len(REL) // 2):
            values = await_blocks(g, p, 1)
            keys = jnp.concatenate([kvb[2 * p, g, 0], kvb[2 * p + 1, g, 0]], axis=0)
            steps = []
            for n, cut in pairs:
                grad = lax.dot_general(values, do8[cut], NT, preferred_element_type=jnp.float32)
                steps.append((prob_s[g, p, :, cut] * (grad - two_rows(delta, n))).astype(jnp.bfloat16))
            steps = jnp.concatenate(steps, axis=1)
            keep(g, p, 0, jnp.dot(steps, q8, preferred_element_type=jnp.float32) * SCALE)
            dq = jnp.dot(keys.T, steps, preferred_element_type=jnp.float32)
            total = dq if total is None else total + dq
        for h in range(GROUP):
            dq_s[:, pl.ds((g * GROUP + h) * HEAD, HEAD)] = (
                total[:, h * TOK:(h + 1) * TOK].T * SCALE
            ).astype(jnp.bfloat16)
        dq_copy(g).start()

    def reorder_columns():
        old = lax.broadcasted_iota(jnp.int32, (1, rows), 1)
        new = old
        before = 0
        for n in range(1, nz * ns):
            shift = (n % ns * nz + n // ns - n) * own_rows
            new = new + jnp.where(old >= n * own_rows, shift - before, 0)
            before = shift
        order = (lax.broadcasted_iota(jnp.int32, (rows, rows), 0) == new).astype(jnp.bfloat16)
        for m in range(1, nxc):
            x_copy(m).wait_recv()

        def reorder(jj, carry):
            two = jnp.concatenate([xg[2 * jj].reshape(rows, TOK), xg[2 * jj + 1].reshape(rows, TOK)], axis=1)
            xp[:, pl.ds(pl.multiple_of(jj * 2 * TOK, 2 * TOK), 2 * TOK)] = jnp.dot(
                order, two, preferred_element_type=jnp.float32
            ).astype(jnp.bfloat16)
            return carry

        lax.fori_loop(0, nxc // 2, reorder, 0)

    def ag_copy(g, m):
        to = lax.rem(i + m, nxc)
        return remote(
            dvall.at[g, i], dvall.at[g, i], ag_ss.at[g, m - 1], ag_rs.at[g, m - 1], dp=zh * nxc + to
        )

    def group_cols(g):
        return pl.ds(pl.multiple_of(g * HEAD, HEAD), HEAD)

    def pass_on(g):
        for c in (4, 5):
            @pl.when(pg_from(c, 0))
            def _():
                pg_copy(g, c, 0)[0].wait_recv()
                mid[c - 4, g] += rb[c - 1, g, 0].astype(jnp.float32)

            sb[c - 3, g, 0] = mid[c - 4, g].astype(jnp.bfloat16)
            pg_send(g, c - 2, 0)

    def settle(half, g):
        for c in (1, 2, 3) if half == 0 else range(1, len(REL)):
            @pl.when(pg_from(c, half))
            def _():
                pg_copy(g, c, half)[0].wait_recv()
                own[g, half] += rb[c - 1, g, half].astype(jnp.float32)
        done = own[g, half].astype(jnp.bfloat16)
        dkv[half, :, group_cols(g)] = done
        if half == 1:
            dvall[g, i] = done
            for m in far_first(nxc):
                ag_copy(g, m).start()

    def rs_copy(g, m):
        to = wrap(s + m)
        return remote(st1.at[g, to], r1.at[g, m - 1], rs_ss.at[g, m - 1], rs_rs.at[g, m - 1], seq=to)

    def weight(g):
        @pl.when(g == 0)
        def _():
            reorder_columns()

        for m in range(1, nxc):
            src = dvall.at[g, lax.rem(i - m + nxc, nxc)]
            remote(src, src, ag_ss.at[g, m - 1], ag_rs.at[g, m - 1], dp=zh * nxc + lax.rem(i + m, nxc)).wait_recv()
        values = dvall[g].reshape(nxc * TOK, HEAD)
        product = jnp.dot(xp[...], values, preferred_element_type=jnp.float32)
        wf[g] = product
        st1[g] = product.astype(jnp.bfloat16).reshape(ns, part, HEAD)
        for m in far_first(ns):
            rs_copy(g, m).start()

    def z_copy(g, m):
        to = lax.rem(zh + m, nz)
        return remote(
            st2.at[g, to], r2.at[g, m - 1], z_ss.at[g, m - 1], z_rs.at[g, m - 1], dp=to * nxc + i
        )

    def sum_seq(g):
        mine = wf[g, pl.ds(pl.multiple_of(s * part, part), part), :]
        for m in range(1, ns):
            rs_copy(g, m).wait_recv()
            mine = mine + r1[g, m - 1].astype(jnp.float32)
        acc[g] = mine
        for n in range(nz):
            st2[g, n, :own_rows, :] = acc[g, n * own_rows:(n + 1) * own_rows, :]
        for m in far_first(nz):
            z_copy(g, m).start()

    def sum_z(g):
        result = st2[g, zh, :own_rows, :]
        for m in range(1, nz):
            z_copy(g, m).wait_recv()
            result = result + r2[g, m - 1, :own_rows, :]
        out_s[:, group_cols(g)] = result * ((ns * nz * nxc * TOK) ** -0.5)

    out_k = pltpu.make_async_copy(dkv.at[0], dk_hbm, out_sem.at[KV])
    out_v = pltpu.make_async_copy(dkv.at[1], dv_hbm, out_sem.at[KV + 1])
    out_w = pltpu.make_async_copy(out_s, dw_hbm, out_sem.at[KV + 2])

    stages = (
        (attend_values, 0),
        (functools.partial(settle, 1), 1),
        (functools.partial(forward, 1), 1),
        (weight, 2),
        (sum_seq, 3),
        (attend_keys, 2),
        (pass_on, 3),
        (functools.partial(settle, 0), 4),
    )

    def step(t, carry):
        @pl.when(t == 1)
        def _():
            lax.fori_loop(0, KV, row_delta, 0)

        for stage, behind in stages:
            @pl.when((t >= behind) & (t < behind + KV))
            def _():
                stage(t - behind)
        return carry

    lax.fori_loop(0, KV + max(behind for _, behind in stages), step, 0)
    out_k.start()
    out_v.start()
    for g in range(KV):
        sum_z(g)
    out_w.start()

    def drain(g, carry):
        for half in range(2):
            for n in range(6):
                copy, wanted = kv_copy(g, n, half)

                @pl.when(wanted)
                def _():
                    copy.wait_send()
            for c in range(1, len(REL)):
                sent, given = pg_copy(g, c, half)

                @pl.when(given)
                def _():
                    sent.wait_send()
        for m in range(1, nxc):
            ag_copy(g, m).wait_send()
        for m in range(1, ns):
            rs_copy(g, m).wait_send()
        for m in range(1, nz):
            z_copy(g, m).wait_send()
        dq_copy(g).wait()
        return carry

    lax.fori_loop(0, KV, drain, 0)
    for m in range(1, nxc):
        x_copy(m).wait_send()
    out_k.wait()
    out_v.wait()
    out_w.wait()


def finish(*refs):
    ins, outs, held, ld, out_sem = refs[:4], refs[4:8], refs[8:12], refs[12], refs[13]
    loads, stores = [], []
    for src, dst, mid in zip(ins, outs, held):
        for col in range(0, src.shape[1], KV * HEAD):
            n, part = len(loads), (slice(None), pl.ds(col, KV * HEAD))
            loads.append(pltpu.make_async_copy(src.at[part], mid.at[part], ld.at[n]))
            stores.append(pltpu.make_async_copy(mid.at[part], dst.at[part], out_sem.at[n]))
    for copy in loads:
        copy.start()
    for copy, store in zip(loads, stores):
        copy.wait()
        store.start()
    for store in stores:
        store.wait()


def solution(mesh, nx=4):
    ns = mesh.shape["seq"]
    nxc = nx * CORES
    nz = mesh.shape["dp"] // nxc

    def on_device(q, k, v, o, do, lse, x, docs, tiles):
        width = x.shape[2]
        own_rows = width // (ns * nz * nxc)
        part = own_rows * nz
        rows = part * ns
        padded = -(-own_rows // 8) * 8
        slots = len(REL)
        bf, f32 = jnp.bfloat16, jnp.float32
        hbm = pl.BlockSpec(memory_space=pl.ANY)
        smem = pl.BlockSpec(memory_space=pltpu.SMEM)
        dma = pltpu.SemaphoreType.DMA
        scratch = [
            pltpu.VMEM((TOK, HQ * HEAD), bf),
            pltpu.VMEM((TOK, HQ * HEAD), bf),
            pltpu.VMEM((TOK, HQ * HEAD), bf),
                        pltpu.VMEM((TOK, width), bf),
            pltpu.VMEM((slots, KV, 2, TOK, HEAD), bf),
            pltpu.VMEM((slots // 2, 2 * TOK, 2 * TOK), f32),
            pltpu.VMEM((HQ, TOK), f32),
            pltpu.VMEM((HQ, TOK), f32),
            pltpu.VMEM((KV, slots // 2, 2 * TOK, GROUP * TOK), f32),
            pltpu.VMEM((TOK, HQ * HEAD), bf),
            pltpu.VMEM((KV, 2, TOK, HEAD), f32),
            pltpu.VMEM((2, KV, TOK, HEAD), f32),
            pltpu.VMEM((slots - 1, KV, 2, TOK, HEAD), bf),
            pltpu.VMEM((slots - 1, KV, 2, TOK, HEAD), bf),
            pltpu.VMEM((2, TOK, KV * HEAD), bf),
            pltpu.VMEM((nz, nxc, rows // nz, TOK), bf),
            pltpu.VMEM((nxc, nz, rows // nz, TOK), bf),
            pltpu.VMEM((rows, nxc * TOK), bf),
            pltpu.VMEM((KV, nxc, TOK, HEAD), bf),
            pltpu.VMEM((KV, rows, HEAD), f32),
            pltpu.VMEM((KV, ns, part, HEAD), bf),
            pltpu.VMEM((KV, ns - 1, part, HEAD), bf),
            pltpu.VMEM((KV, part, HEAD), f32),
            pltpu.VMEM((KV, nz, padded, HEAD), f32),
            pltpu.VMEM((KV, max(nz - 1, 1), padded, HEAD), f32),
            pltpu.VMEM((own_rows, KV * HEAD), f32),
            dma((KV, 2)),
            dma((5,)),
            dma((KV + 3,)),
            dma((slots, KV, 2)),
            dma((slots - 1, KV, 2)),
            dma((slots - 1, KV, 2)),
            dma((slots - 1, KV, 2)),
            dma((nxc - 1,)),
            dma((nxc - 1,)),
            dma((KV, nxc - 1)),
            dma((KV, nxc - 1)),
            dma((KV, ns - 1)),
            dma((KV, ns - 1)),
            dma((KV, max(nz - 1, 1))),
            dma((KV, max(nz - 1, 1))),
        ]
        shapes = (
            jax.ShapeDtypeStruct((TOK, HQ * HEAD), bf),
            jax.ShapeDtypeStruct((TOK, KV * HEAD), bf),
            jax.ShapeDtypeStruct((TOK, KV * HEAD), bf),
            jax.ShapeDtypeStruct((own_rows, KV * HEAD), f32),
        )
        results = pl.pallas_call(
            functools.partial(kernel, nx, nz, ns),
            out_shape=shapes,
            in_specs=[smem, smem] + [hbm] * 7,
            out_specs=(hbm,) * 4,
            scratch_shapes=scratch,
            compiler_params=pltpu.CompilerParams(
                collective_id=0, has_side_effects=True, vmem_limit_bytes=60 * 2**20
            ),
        )(docs, tiles, q[0], k[0], v[0], o[0], do[0], lse[0].T, x[0])
        dq, dk, dv, dw = pl.pallas_call(
            finish,
            out_shape=shapes,
            in_specs=[hbm] * 4,
            out_specs=(hbm,) * 4,
            scratch_shapes=[pltpu.VMEM(a.shape, a.dtype) for a in shapes] + [dma((GROUP + 3,))] * 2,
            compiler_params=pltpu.CompilerParams(vmem_limit_bytes=60 * 2**20),
        )(*results)
        return dq[None], dk[None], dv[None], dw

    split = P("dp", "seq", None)
    return jax.shard_map(
        on_device,
        mesh=mesh,
        in_specs=(split,) * 7 + (P("dp", None),) * 2,
        out_specs=(split,) * 3 + (P(("dp", "seq"), None),),
        check_vma=False,
    )
```
